512 devices in a mesh: orb: 64 (over x, z), comp: 8 (over y, core).
Axes of the slice: x: 4, y: 4, z: 16, core: 2. Of those that a mesh axis runs over, the one named last changes fastest.
Arguments:
- orbitals: float32 [64, 128, 128, 128], P('orb', 'comp'), may hold values from -24 to 24
- potential: float32 [128, 128, 128], P('comp'), may hold values from 0.1 to 4
- segments: int32 [2, 128, 128], P(None, 'comp'), may hold values from 0 to 128, as said below
Outputs:
- new_orbitals: float32 [64, 128, 128, 128], P('orb', 'comp')
- grad_rms: float32 [64], replicated
The draws below stay inside these ranges and needn't reach their ends.
Inputs may be any that keep to these rules, and one draw needn't show every extreme that they name: segments[0] <= segments[1] in every column, and each region holds at least 64 cells.
All inputs are finite; a program needn't handle non-finite values.
Results may differ from the reference program's by a relative error of at most 0.00007.
Values sent between devices are 32-bit elements; how exact they have to be, the bound alone decides.
No kernel may reach another device: no remote copies, remote signals or barrier semaphores. Data moves between devices by JAX's collectives and lax.ppermute only.
A program may use at most 64 MiB of HBM per device.

```python
import math
import jax
import jax.numpy as jnp
from jax import lax

NY = 128
NZ = 128
NORB = 64
NX = 128


def draw_segments(key, part):
    key = jax.random.fold_in(key, 11)
    first_key, second_key = jax.random.split(key)
    starts = jax.random.randint(first_key, (NX, NY), 0, NZ // 4, dtype=jnp.int32)
    spans = jax.random.randint(second_key, (NX, NY), NZ // 2, NZ // 2 + NZ // 4 + 1, dtype=jnp.int32)
    return jnp.stack([starts, starts + spans]).astype(jnp.int32)


def draw_orbitals(key, part):
    key = jax.random.fold_in(key, 5)
    field_key = jax.random.fold_in(key, 1)
    mixing_key = jax.random.fold_in(key, 2)
    noise_key = jax.random.fold_in(key, 3)
    fields = jnp.clip(jax.random.normal(field_key, (4, NX, NY, NZ), jnp.float32), -6.0, 6.0)
    mixing = jnp.clip(0.15 * jax.random.normal(mixing_key, (NORB, 4), jnp.float32), -0.6, 0.6)
    own_noise = jnp.clip(jax.random.normal(noise_key, (NORB, NX, NY, NZ), jnp.float32), -6.0, 6.0)
    result = own_noise
    for field_index in range(4):
        result = result + mixing[:, field_index, None, None, None] * fields[field_index][None]
    return result.astype(jnp.float32)


def level_of(stream_key, extent, cuts, smallest, high):
    def one(dim, shards_of):
        steps = jax.random.uniform(jax.random.fold_in(jax.random.fold_in(stream_key, 6), dim), (shards_of,), jnp.float32, smallest / len(cuts), high / len(cuts))
        return jnp.repeat(jnp.exp(steps), extent[dim] // shards_of).reshape((-1,) + (1,) * (len(extent) - dim - 1))

    gain = one(*cuts[0])
    for cut in cuts[1:]:
        gain = gain * one(*cut)
    return gain


def setup_inputs(seed: int = 0) -> dict:
    arg_keys = jax.random.split(jax.random.key(seed), 4)
    orbitals = draw_orbitals(jax.random.fold_in(arg_keys[3], 71), 0)
    potential = jnp.clip(jnp.exp(math.log(4.0) - 3.6888794 * jax.random.uniform(arg_keys[1], (NX, NY, NZ), jnp.float32) ** level_of(arg_keys[1], (NX, NY, NZ), ((0, 8),), -0.2, 0.2)), 0.1, 4.0)
    segments = draw_segments(jax.random.fold_in(arg_keys[3], 71), 0)
    return {"orbitals": orbitals, "potential": potential, "segments": segments}


spacing = 0.4
descent = 0.02

def second_coefs_list():
    accuracy_order = 7
    coef_terms = []
    for offset in range(1, accuracy_order + 1):
        coef_terms.append(2.0 * (-1) ** (offset + 1) * math.factorial(accuracy_order) ** 2 / (offset * offset * math.factorial(accuracy_order - offset) * math.factorial(accuracy_order + offset)))
    return [-2.0 * sum(coef_terms)] + coef_terms

def convolve(orbital, axis_index):
    stencil = second_coefs_list()
    halo_width = len(stencil) - 1
    pads = [(0, 0), (0, 0), (0, 0)]
    pads[axis_index] = (halo_width, halo_width)
    padded = jnp.pad(orbital, pads)
    extent_len = orbital.shape[axis_index]
    summed = stencil[0] * orbital
    for offset in range(1, halo_width + 1):
        upper_part = lax.slice_in_dim(padded, halo_width + offset, halo_width + offset + extent_len, axis=axis_index)
        lower_part = lax.slice_in_dim(padded, halo_width - offset, halo_width - offset + extent_len, axis=axis_index)
        summed = summed + stencil[offset] * (upper_part + lower_part)
    return summed

def hamiltonian(orbital, potential):
    laplace = convolve(orbital, 0) + convolve(orbital, 1) + convolve(orbital, 2)
    return -0.5 / spacing ** 2 * laplace + potential * orbital

def reference(orbitals, potential, segments):
    images = lax.map(lambda single: hamiltonian(single, potential), orbitals)
    orbital_count = orbitals.shape[0]
    flat_orbitals = orbitals.reshape(orbital_count, -1)
    flat_images = images.reshape(orbital_count, -1)
    cell_total = flat_orbitals.shape[1]
    correlation = jnp.dot(flat_orbitals, flat_images.T, precision=lax.Precision.HIGHEST) / cell_total
    lagrange = 0.5 * (correlation + correlation.T)
    gradient = flat_images - jnp.dot(lagrange, flat_orbitals, precision=lax.Precision.HIGHEST)
    squares = lax.optimization_barrier(jnp.sum(gradient * gradient, axis=1))
    grad_rms = jnp.sqrt(squares / cell_total)
    depth_index = jnp.arange(NZ, dtype=jnp.int32)
    inside = (depth_index >= segments[0][..., None]) & (depth_index < segments[1][..., None])
    updated = (flat_orbitals - descent * gradient).reshape(orbitals.shape)
    new_orbitals = jnp.where(inside[None], updated, jnp.float32(0.0))
    return (new_orbitals, grad_rms)
```

```python
import functools
import math

import jax
import jax.numpy as jnp
import numpy as np
from jax import lax
from jax.experimental import pallas as pl
from jax.experimental.pallas import tpu as pltpu
from jax.sharding import Mesh
from jax.sharding import PartitionSpec as P

spacing = 0.4
descent = 0.02
NX, NY, NZ, NORB = 128, 128, 128, 64
CELLS = NX * NY * NZ
KINETIC = -0.5 / spacing**2
REACH = 7
XG, YB, XL, ZB = 4, 8, 4, 32
ROWS, LANES = XG * YB, XL * ZB
HIGH = lax.Precision.HIGHEST
PARAMS = pltpu.CompilerParams(vmem_limit_bytes=48 * 1024 * 1024)
ORB, COMP = ("x", "z"), ("y", "core")


def second_coefs_list():
    terms = []
    for k in range(1, REACH + 1):
        terms.append(
            2.0
            * (-1) ** (k + 1)
            * math.factorial(REACH) ** 2
            / (k * k * math.factorial(REACH - k) * math.factorial(REACH + k))
        )
    return [-2.0 * sum(terms)] + terms


COEFS = [KINETIC * c for c in second_coefs_list()]


def lane_matrices(forward):
    own, near, far = (np.zeros((LANES, LANES)) for _ in range(3))
    halo = np.zeros((XG, LANES, LANES))

    def coef(k):
        return COEFS[k] if 1 <= k <= REACH else 0.0

    for x in range(XL):
        for z in range(ZB):
            out = x * ZB + z
            for zi in range(ZB):
                own[x * ZB + zi, out] += coef(zi - z if forward else z - zi)
            for xi in range(XL):
                step = xi - x if forward else x - xi
                own[xi * ZB + z, out] += coef(step)
                near[xi * ZB + z, out] += coef(step + XL)
                far[xi * ZB + z, out] += coef(step + 2 * XL)
            for xg in range(XG):
                for t in range(8):
                    k = ZB + t - z if forward else z + 8 - t
                    halo[xg, x * ZB + xg * 8 + t, out] += coef(k)
    first = np.concatenate([own, near], axis=0)
    second = np.stack([np.concatenate([far, halo[xg]], axis=0) for xg in range(XG)])
    return first.astype(np.float32), second.astype(np.float32)


def pack_kernel(src, dst):
    group = lax.broadcasted_iota(jnp.int32, (32, LANES), 1) // ZB
    for xg in range(XG):
        for part in range(4):
            rows = slice(part * 32, part * 32 + 32)
            layers = [src[xg * XL + x, rows, :] for x in range(XL)]
            for q in range(4):
                piece = layers[q]
                for x in range(XL):
                    if x != q:
                        moved = pltpu.roll(layers[x], ((x - q) * ZB) % LANES, 1)
                        piece = jnp.where(group == x, moved, piece)
                first = q * 16 + part * 4
                dst[first : first + 4, xg * YB : (xg + 1) * YB, :] = piece.reshape(4, YB, LANES)


def unpack_kernel(src, dst):
    group = lax.broadcasted_iota(jnp.int32, (YB, LANES), 1) // ZB
    for yb in range(16):
        for xg in range(XG):
            pieces = [src[pl.ds((q * 16 + yb) * (ROWS + 1) + xg * YB, YB), :] for q in range(4)]
            for x in range(XL):
                layer = pieces[x]
                for q in range(4):
                    if q != x:
                        moved = pltpu.roll(pieces[q], ((q - x) * ZB) % LANES, 1)
                        layer = jnp.where(group == q, moved, layer)
                dst[xg * XL + x, yb * YB : (yb + 1) * YB, :] = layer


def spread_kernel(src, phi, y_up_a, y_down_b, x_up, z_up, y_down_a, y_up_b, x_down, z_down):
    slot = (lax.broadcasted_iota(jnp.int32, (NORB, LANES), 1) % ZB) // 8
    for y in range(YB):
        up = down = jnp.zeros((NORB, LANES), jnp.float32)
        for xg in range(XG):
            r = xg * YB + y
            row = src[pl.ds(r, NORB, stride=ROWS), :]
            phi[r] = row
            g = xg % 2
            if xg < 2:
                x_up[r] = row
                if y < REACH:
                    y_up_a[g * REACH + y] = row
                if y >= 1:
                    y_down_a[g * REACH + y - 1] = row
            else:
                x_down[r - 2 * YB] = row
                if y < REACH:
                    y_up_b[g * REACH + y] = row
                if y >= 1:
                    y_down_b[g * REACH + y - 1] = row
            up = jnp.where(slot == xg, pltpu.roll(row, xg * 8, 1) if xg else row, up)
            down = jnp.where(slot == xg, pltpu.roll(row, (xg * 8 - 24) % LANES, 1) if xg != 3 else row, down)
        z_up[y] = up
        z_down[y] = down


def one_side(forward, xg, phi, y_halo, y_forward, x_halo, z_halo, half, first, second):
    def group(i):
        if 0 <= i < XG:
            return phi[i * YB : (i + 1) * YB].reshape(YB * NORB, LANES)
        j = i - XG if forward else i + 2
        return x_halo[j * YB : (j + 1) * YB].reshape(YB * NORB, LANES)

    step = 1 if forward else -1
    lhs = jnp.concatenate([group(xg), group(xg + step)], axis=1)
    total = jnp.dot(lhs, first[...], precision=HIGH, preferred_element_type=jnp.float32)
    lhs = jnp.concatenate([group(xg + 2 * step), z_halo[...].reshape(YB * NORB, LANES)], axis=1)
    total = total + jnp.dot(lhs, second[xg], precision=HIGH, preferred_element_type=jnp.float32)
    g = xg % 2
    result = []
    for y in range(YB):
        r = xg * YB + y
        value = total[y * NORB : (y + 1) * NORB] + half[r : r + 1, :] * phi[r]
        for k in range(1, REACH + 1):
            if y_forward:
                row = phi[r + k] if y + k < YB else y_halo[g * REACH + y + k - YB]
            else:
                row = phi[r - k] if y - k >= 0 else y_halo[g * REACH + REACH + y - k]
            value = value + COEFS[k] * row
        result.append(value)
    return result


def first_side_kernel(phi, y_a, y_b, x_halo, z_halo, half, first, second, out, partial):
    total = jnp.zeros((NORB, NORB), jnp.float32)
    for xg in range(XG):
        y_halo = y_a if xg < 2 else y_b
        values = one_side(True, xg, phi, y_halo, xg < 2, x_halo, z_halo, half, first, second)
        for y in range(YB):
            out[xg * YB + y] = values[y]
        left = jnp.concatenate([phi[xg * YB + y] for y in range(YB)], axis=1)
        right = jnp.concatenate(values, axis=1)
        total = total + lax.dot_general(
            left, right, (((1,), (1,)), ((), ())), precision=HIGH, preferred_element_type=jnp.float32
        )
    partial[...] = jnp.concatenate([total[: NORB // 2], total[NORB // 2 :]], axis=1)


def second_side_kernel(phi, y_a, y_b, x_halo, z_halo, half, first, second, before, out):
    for xg in range(XG):
        y_halo = y_a if xg < 2 else y_b
        values = one_side(False, xg, phi, y_halo, xg >= 2, x_halo, z_halo, half, first, second)
        for y in range(YB):
            r = xg * YB + y
            out[r] = before[r] + values[y]


def update_kernel(phi, images, lagrange, inside, out):
    lag = lagrange[...]
    squares = jnp.zeros((NORB, LANES), jnp.float32)
    for xg in range(XG):
        rows = [phi[xg * YB + y] for y in range(YB)]
        mixed = jnp.dot(lag, jnp.concatenate(rows, axis=1), precision=HIGH, preferred_element_type=jnp.float32)
        for y in range(YB):
            r = xg * YB + y
            gradient = images[r] - mixed[:, y * LANES : (y + 1) * LANES]
            squares = squares + gradient * gradient
            moved = rows[y] - descent * gradient
            out[pl.ds(r, NORB, stride=ROWS + 1), :] = jnp.where(inside[r : r + 1, :] > 0.0, moved, 0.0)
    ones = jnp.ones((8, LANES), jnp.float32)
    sums = lax.dot_general(ones, squares, (((1,), (1,)), ((), ())), precision=HIGH, preferred_element_type=jnp.float32)
    sums = jnp.concatenate([sums, jnp.zeros((8, LANES - NORB), jnp.float32)], axis=1)
    out[pl.ds(ROWS, NORB, stride=ROWS + 1), :] = jnp.broadcast_to(sums[0:1, :], (NORB, LANES))


def f32(*shape):
    return jax.ShapeDtypeStruct(shape, jnp.float32)


def call(kernel, out_shape, name, flops, nbytes):
    return pl.pallas_call(
        kernel,
        out_shape=out_shape,
        compiler_params=PARAMS,
        name=name,
        cost_estimate=pl.CostEstimate(flops=flops, bytes_accessed=nbytes, transcendentals=0),
    )


def copies_sum(value, axes):
    peers = math.prod(lax.axis_size(a) for a in axes)
    sent = jnp.broadcast_to(value[None], (peers,) + value.shape)
    return jnp.sum(lax.all_to_all(sent, axes, 0, 0, tiled=True), axis=0)


def shift(value, axes, count, up):
    pairs = [(i + 1, i) if up else (i, i + 1) for i in range(count - 1)]
    return lax.ppermute(value, axes, pairs)


def on_device(orbitals, potential, segments):
    mib = 1 << 20
    with jax.named_scope("pack"):
        pieces = call(pack_kernel, f32(NORB, ROWS, LANES), "pack", 1 << 20, 2 * mib)(orbitals[0])
    with jax.named_scope("transpose"):
        arrived = lax.all_to_all(pieces, ORB, 0, 0, tiled=True).reshape(NORB * ROWS, LANES)

    x_pos, z_pos = lax.axis_index("x"), lax.axis_index("z")
    with jax.named_scope("block_constants"):
        block = lax.dynamic_slice(potential, (0, z_pos * YB, x_pos * ZB), (16, YB, ZB))
        block = block.reshape(XG, XL, YB, ZB).transpose(0, 2, 1, 3).reshape(ROWS, LANES)
        half = 0.5 * (jnp.float32(3.0 * COEFS[0]) + block)
        ends = lax.dynamic_slice(segments, (0, 0, z_pos * YB), (2, 16, YB))
        ends = ends.reshape(2, XG, XL, YB).transpose(0, 1, 3, 2)
        ends = jnp.broadcast_to(ends[..., None], (2, XG, YB, XL, ZB)).reshape(2, ROWS, LANES)
        depth = x_pos * ZB + lax.broadcasted_iota(jnp.int32, (ROWS, LANES), 1) % ZB
        inside = ((depth >= ends[0]) & (depth < ends[1])).astype(jnp.float32)
    up_first, up_second = (jnp.asarray(m) for m in lane_matrices(True))
    down_first, down_second = (jnp.asarray(m) for m in lane_matrices(False))

    with jax.named_scope("spread"):
        y_shape, x_shape, z_shape = (f32(2 * REACH, NORB, LANES), f32(2 * YB, NORB, LANES), f32(YB, NORB, LANES))
        side = [y_shape, y_shape, x_shape, z_shape]
        phi, *sides = call(spread_kernel, [f32(ROWS, NORB, LANES)] + side + side, "spread", 1 << 20, 6 * mib)(arrived)
    y_up_a, y_down_b, x_up, z_up, y_down_a, y_up_b, x_down, z_down = sides
    with jax.named_scope("first_halo"):
        y_up_a = shift(y_up_a, "z", 16, True)
        y_down_b = shift(y_down_b, "z", 16, False)
        x_up = shift(x_up, COMP, 8, True)
        z_up = shift(z_up, "x", 4, True)
    with jax.named_scope("first_side"):
        one, partial = call(
            first_side_kernel, [f32(ROWS, NORB, LANES), f32(NORB // 2, 2 * NORB)], "first_side", 1 << 30, 5 * mib
        )(phi, y_up_a, y_down_b, x_up, z_up, half, up_first, up_second)
    with jax.named_scope("correlation_sum"):
        partial = copies_sum(partial, ("x", "y"))
        partial = copies_sum(partial, ("core",))
        partial = copies_sum(partial, ("z",))
        partial = jnp.concatenate([partial[:, :NORB], partial[:, NORB:]], axis=0)
        lagrange = (partial + partial.T) * jnp.float32(1.0 / CELLS)
    with jax.named_scope("second_halo"):
        y_down_a = shift(y_down_a, "z", 16, False)
        y_up_b = shift(y_up_b, "z", 16, True)
        x_down = shift(x_down, COMP, 8, False)
        z_down = shift(z_down, "x", 4, False)
    with jax.named_scope("second_side"):
        images = call(second_side_kernel, f32(ROWS, NORB, LANES), "second_side", 1 << 30, 6 * mib)(
            phi, y_down_a, y_up_b, x_down, z_down, half, down_first, down_second, one
        )
    with jax.named_scope("update"):
        sent = call(update_kernel, f32(NORB * (ROWS + 1), LANES), "update", 1 << 28, 3 * mib)(
            phi, images, lagrange, inside
        )
    with jax.named_scope("transpose_back"):
        back = lax.all_to_all(sent.reshape(NORB, ROWS + 1, 1, LANES), ORB, 0, 0, tiled=True)
    with jax.named_scope("rms"):
        slab = jnp.sum(back[:, ROWS, :, :], axis=0)
        squares = copies_sum(slab, COMP)[0, :NORB]
        grad_rms = jnp.sqrt(squares / CELLS)
    with jax.named_scope("unpack"):
        new = call(unpack_kernel, f32(16, NY, NZ), "unpack", 1 << 20, 2 * mib)(back.reshape(NORB * (ROWS + 1), LANES))
    return new[None], grad_rms


def solution(mesh):
    fine = Mesh(mesh.devices.reshape(4, 16, 4, 2), ("x", "z", "y", "core"))
    return jax.shard_map(
        on_device,
        mesh=fine,
        in_specs=(P(ORB, COMP, None, None), P(COMP, None, None), P(None, COMP, None)),
        out_specs=(P(ORB, COMP, None, None), P()),
        check_vma=False,
    )
```

```python
import math

import jax
import jax.numpy as jnp
import numpy as np
from jax import lax
from jax.experimental import pallas as pl
from jax.experimental.pallas import tpu as pltpu
from jax.sharding import Mesh
from jax.sharding import PartitionSpec as P

spacing = 0.4
descent = 0.02
NX, NY, NZ, NORB = 128, 128, 128, 64
CELLS = NX * NY * NZ
KINETIC = -0.5 / spacing**2
REACH = 7
XG, YB, XL, ZB = 4, 8, 4, 32
ROWS, LANES = XG * YB, XL * ZB
HIGH = lax.Precision.HIGHEST
PARAMS = pltpu.CompilerParams(vmem_limit_bytes=12 * 1024 * 1024)
ORB, COMP = ("x", "z"), ("y", "core")


def second_coefs_list():
    terms = []
    for k in range(1, REACH + 1):
        terms.append(
            2.0
            * (-1) ** (k + 1)
            * math.factorial(REACH) ** 2
            / (k * k * math.factorial(REACH - k) * math.factorial(REACH + k))
        )
    return [-2.0 * sum(terms)] + terms


COEFS = [KINETIC * c for c in second_coefs_list()]


def coef(k):
    return COEFS[k] if 1 <= k <= REACH else 0.0


def inner_matrix():
    x, z = 16, ZB
    line_x = np.array([[coef(abs(i - j)) for j in range(x)] for i in range(x)])
    line_z = np.array([[coef(abs(i - j)) for j in range(z)] for i in range(z)])
    return (np.kron(line_x, np.eye(z)) + np.kron(np.eye(x), line_z)).astype(np.float32)


def edge_matrix(forward):
    table = np.zeros((3 * LANES, XG * LANES))
    for x in range(16):
        for z in range(ZB):
            out = x * ZB + z
            for layer in range(8):
                table[layer * ZB + z, out] += coef(16 + layer - x if forward else x + 8 - layer)
            for t in range(8):
                row = 2 * LANES + (x % XL) * ZB + (x // XL) * 8 + t
                table[row, out] += coef(ZB + t - z if forward else z + 8 - t)
    return table.astype(np.float32)


def pack_kernel(src, dst):
    group = lax.broadcasted_iota(jnp.int32, (32, LANES), 1) // ZB
    for xg in range(XG):
        for part in range(4):
            rows = slice(part * 32, part * 32 + 32)
            layers = [src[xg * XL + x, rows, :] for x in range(XL)]
            for q in range(4):
                piece = layers[q]
                for x in range(XL):
                    if x != q:
                        moved = pltpu.roll(layers[x], ((x - q) * ZB) % LANES, 1)
                        piece = jnp.where(group == x, moved, piece)
                first = q * 16 + part * 4
                dst[first : first + 4, xg * YB : (xg + 1) * YB, :] = piece.reshape(4, YB, LANES)


def unpack_kernel(src, dst):
    group = lax.broadcasted_iota(jnp.int32, (YB, LANES), 1) // ZB
    for yb in range(16):
        for xg in range(XG):
            pieces = [src[pl.ds((q * 16 + yb) * (ROWS + 1) + xg * YB, YB), :] for q in range(4)]
            for x in range(XL):
                layer = pieces[x]
                for q in range(4):
                    if q != x:
                        moved = pltpu.roll(pieces[q], ((q - x) * ZB) % LANES, 1)
                        layer = jnp.where(group == q, moved, layer)
                dst[xg * XL + x, yb * YB : (yb + 1) * YB, :] = layer


def spread_kernel(src, phi, y_up_a, y_down_b, x_up, z_up, y_down_a, y_up_b, x_down, z_down):
    slot = (lax.broadcasted_iota(jnp.int32, (NORB, LANES), 1) % ZB) // 8
    for y in range(YB):
        up = down = jnp.zeros((NORB, LANES), jnp.float32)
        for xg in range(XG):
            r = xg * YB + y
            row = src[pl.ds(r, NORB, stride=ROWS), :]
            phi[r] = row
            g = xg % 2
            if xg < 2:
                x_up[r] = row
                if y < REACH:
                    y_up_a[g * REACH + y] = row
                if y >= 1:
                    y_down_a[g * REACH + y - 1] = row
            else:
                x_down[r - 2 * YB] = row
                if y < REACH:
                    y_up_b[g * REACH + y] = row
                if y >= 1:
                    y_down_b[g * REACH + y - 1] = row
            up = jnp.where(slot == xg, pltpu.roll(row, xg * 8, 1) if xg else row, up)
            down = jnp.where(slot == xg, pltpu.roll(row, (xg * 8 - 24) % LANES, 1) if xg != 3 else row, down)
        z_up[y] = up
        z_down[y] = down


def constants_kernel(place, potential, segments, diagonal, inside):
    x_pos, z_pos = place[0], place[1]
    lane = lax.broadcasted_iota(jnp.int32, (YB, LANES), 1)
    first_row = pl.multiple_of(z_pos * YB, YB)
    pick = lax.broadcasted_iota(jnp.int32, (YB, NY), 1) == z_pos * YB + lax.broadcasted_iota(jnp.int32, (YB, NY), 0)
    ends = []
    for side in range(2):
        table = segments[side].astype(jnp.float32)
        ends.append(
            lax.dot_general(
                pick.astype(jnp.float32), table, (((1,), (1,)), ((), ())), precision=HIGH, preferred_element_type=jnp.float32
            )
        )
    depth = (x_pos * ZB + lane % ZB).astype(jnp.float32)
    layer = lax.broadcasted_iota(jnp.int32, (16, LANES), 0)
    for xg in range(XG):
        block = jnp.zeros((YB, LANES), jnp.float32)
        for x in range(XL):
            rows = potential[xg * XL + x, pl.ds(first_row, YB), :]
            moved = pltpu.roll(rows, lax.rem(x * ZB + LANES - x_pos * ZB, LANES), 1)
            block = jnp.where(lane // ZB == x, moved, block)
        diagonal[xg * YB : (xg + 1) * YB, :] = block + jnp.float32(3.0 * COEFS[0])
        widen = layer == xg * XL + lax.broadcasted_iota(jnp.int32, (16, LANES), 1) // ZB
        low, high = (
            jnp.dot(e, widen.astype(jnp.float32), precision=HIGH, preferred_element_type=jnp.float32) for e in ends
        )
        held = jnp.where(depth >= low, 1.0, 0.0) * jnp.where(depth < high, 1.0, 0.0)
        inside[xg * YB : (xg + 1) * YB, :] = held


def tall(ref, xg):
    return ref[xg * YB : (xg + 1) * YB].reshape(YB * NORB, LANES)


def pair_sums(left, right):
    left, right = jnp.concatenate(left, axis=1), jnp.concatenate(right, axis=1)
    return lax.dot_general(
        left, right, (((1,), (1,)), ((), ())), precision=HIGH, preferred_element_type=jnp.float32
    )


def inner_kernel(phi, diagonal, matrix, images, half_sums):
    total = jnp.zeros((NORB, NORB), jnp.float32)
    for pair in range(2):
        cells = jnp.concatenate([tall(phi, xg) for xg in range(XG)], axis=1)
        columns = slice(pair * 2 * LANES, (pair + 1) * 2 * LANES)
        both = jnp.dot(cells, matrix[:, columns], precision=HIGH, preferred_element_type=jnp.float32)
        for xg in (2 * pair, 2 * pair + 1):
            own = slice((xg % 2) * LANES, (xg % 2 + 1) * LANES)
            rows = [phi[xg * YB + y] for y in range(YB)]
            values = []
            for y in range(YB):
                r = xg * YB + y
                value = both[y * NORB : (y + 1) * NORB, own] + diagonal[r : r + 1, :] * rows[y]
                for other in range(YB):
                    if other != y:
                        value = value + COEFS[abs(other - y)] * rows[other]
                images[r] = value
                values.append(value)
            total = total + pair_sums(rows, values)
    half_sums[...] = 0.5 * total


def edge_terms(forward, x_halo, z_halo, y_a, y_b, matrix):
    halo = jnp.concatenate([tall(x_halo, 0), tall(x_halo, 1), z_halo[...].reshape(YB * NORB, LANES)], axis=1)
    for pair in range(2):
        columns = slice(pair * 2 * LANES, (pair + 1) * 2 * LANES)
        both = jnp.dot(halo, matrix[:, columns], precision=HIGH, preferred_element_type=jnp.float32)
        y_halo = y_b if pair else y_a
        for xg in (2 * pair, 2 * pair + 1):
            own = slice((xg % 2) * LANES, (xg % 2 + 1) * LANES)
            rows = [y_halo[(xg % 2) * REACH + i] for i in range(REACH)]
            values = []
            for y in range(YB):
                value = both[y * NORB : (y + 1) * NORB, own]
                for i in range(REACH):
                    k = YB + i - y if forward != bool(pair) else y + REACH - i
                    if 1 <= k <= REACH:
                        value = value + COEFS[k] * rows[i]
                values.append(value)
            yield xg, values


def first_edge_kernel(phi, y_a, y_b, x_halo, z_halo, matrix, inner, half_sums, images, partial):
    total = half_sums[...]
    for xg, values in edge_terms(True, x_halo, z_halo, y_a, y_b, matrix):
        for y in range(YB):
            images[xg * YB + y] = inner[xg * YB + y] + values[y]
        total = total + pair_sums([phi[xg * YB + y] for y in range(YB)], values)
    partial[...] = jnp.concatenate([total[: NORB // 2], total[NORB // 2 :]], axis=1)


def second_edge_kernel(y_a, y_b, x_halo, z_halo, matrix, before, images):
    for xg, values in edge_terms(False, x_halo, z_halo, y_a, y_b, matrix):
        for y in range(YB):
            images[xg * YB + y] = before[xg * YB + y] + values[y]


def update_kernel(phi, images, sums, inside, out):
    packed = jnp.sum(sums[...], axis=0)
    half = jnp.concatenate([packed[:, :NORB], packed[:, NORB:]], axis=0)
    lag = (half + half.T) * jnp.float32(1.0 / CELLS)
    squares = jnp.zeros((NORB, LANES), jnp.float32)
    for xg in range(XG):
        rows = [phi[xg * YB + y] for y in range(YB)]
        mixed = jnp.dot(lag, jnp.concatenate(rows, axis=1), precision=HIGH, preferred_element_type=jnp.float32)
        for y in range(YB):
            r = xg * YB + y
            gradient = images[r] - mixed[:, y * LANES : (y + 1) * LANES]
            squares = squares + gradient * gradient
            moved = rows[y] - descent * gradient
            out[pl.ds(r, NORB, stride=ROWS + 1), :] = jnp.where(inside[r : r + 1, :] > 0.0, moved, 0.0)
    ones = jnp.ones((8, LANES), jnp.float32)
    sums = lax.dot_general(ones, squares, (((1,), (1,)), ((), ())), precision=HIGH, preferred_element_type=jnp.float32)
    sums = jnp.concatenate([sums, jnp.zeros((8, LANES - NORB), jnp.float32)], axis=1)
    out[pl.ds(ROWS, NORB, stride=ROWS + 1), :] = jnp.broadcast_to(sums[0:1, :], (NORB, LANES))


def f32(*shape):
    return jax.ShapeDtypeStruct(shape, jnp.float32)


def call(kernel, out_shape, name, flops, nbytes, **more):
    return pl.pallas_call(
        kernel,
        out_shape=out_shape,
        compiler_params=PARAMS,
        name=name,
        cost_estimate=pl.CostEstimate(flops=flops, bytes_accessed=nbytes, transcendentals=0),
        **more,
    )


def copies(value, axes):
    peers = math.prod(lax.axis_size(a) for a in axes)
    sent = jnp.broadcast_to(value[None], (peers,) + value.shape)
    return lax.all_to_all(sent, axes, 0, 0, tiled=True)


def shift(value, axes, count, up):
    pairs = [(i + 1, i) if up else (i, i + 1) for i in range(count - 1)]
    return lax.ppermute(value, axes, pairs)


def on_device(orbitals, potential, segments):
    mib = 1 << 20
    with jax.named_scope("pack"):
        pieces = call(pack_kernel, f32(NORB, ROWS, LANES), "pack", 1 << 20, 2 * mib)(orbitals[0])
    with jax.named_scope("transpose"):
        arrived = lax.all_to_all(pieces, ORB, 0, 0, tiled=True).reshape(NORB * ROWS, LANES)

    with jax.named_scope("block_constants"):
        place = jnp.stack([lax.axis_index("x"), lax.axis_index("z")]).astype(jnp.int32)
        vmem = pl.BlockSpec(memory_space=pltpu.VMEM)
        diagonal, inside = call(
            constants_kernel,
            [f32(ROWS, LANES)] * 2,
            "constants",
            1 << 20,
            mib,
            in_specs=[pl.BlockSpec(memory_space=pltpu.SMEM), vmem, vmem],
        )(place, potential, segments)
    inner, ahead, behind = (jnp.asarray(m) for m in (inner_matrix(), edge_matrix(True), edge_matrix(False)))

    with jax.named_scope("spread"):
        side = [f32(2 * REACH, NORB, LANES)] * 2 + [f32(2 * YB, NORB, LANES), f32(YB, NORB, LANES)]
        whole = f32(ROWS, NORB, LANES)
        phi, *sides = call(spread_kernel, [whole] + side + side, "spread", 1 << 20, 6 * mib)(arrived)
    y_up_a, y_down_b, x_up, z_up, *second = sides
    with jax.named_scope("first_halo"):
        y_up_a = shift(y_up_a, "z", 16, True)
        y_down_b = shift(y_down_b, "z", 16, False)
        x_up = shift(x_up, COMP, 8, True)
        z_up = shift(z_up, "x", 4, True)
    with jax.named_scope("inner"):
        images, sums = call(inner_kernel, [whole, f32(NORB, NORB)], "inner", 1 << 32, 2 * mib)(phi, diagonal, inner)
    with jax.named_scope("first_edge"):
        images, partial = call(first_edge_kernel, [whole, f32(NORB // 2, 2 * NORB)], "first_edge", 1 << 31, 4 * mib)(
            phi, y_up_a, y_down_b, x_up, z_up, ahead, images, sums
        )
    partial, second = lax.optimization_barrier((partial, second))
    y_down_a, y_up_b, x_down, z_down = second
    with jax.named_scope("correlation_sum"):
        partial = jnp.sum(copies(partial, ("x", "y")), axis=0)
        partial = jnp.sum(copies(partial, ("core",)), axis=0)
    with jax.named_scope("second_halo"):
        y_down_a = shift(y_down_a, "z", 16, False)
        y_up_b = shift(y_up_b, "z", 16, True)
        x_down = shift(x_down, COMP, 8, False)
        z_down = shift(z_down, "x", 4, False)
    partial, y_down_a, y_up_b, x_down, z_down = lax.optimization_barrier((partial, y_down_a, y_up_b, x_down, z_down))
    with jax.named_scope("correlation_sum"):
        partial = copies(partial, ("z",))
    with jax.named_scope("second_edge"):
        images = call(second_edge_kernel, whole, "second_edge", 1 << 31, 4 * mib)(
            y_down_a, y_up_b, x_down, z_down, behind, images
        )
    with jax.named_scope("update"):
        sent = call(update_kernel, f32(NORB * (ROWS + 1), LANES), "update", 1 << 28, 3 * mib)(
            phi, images, partial, inside
        )
    with jax.named_scope("transpose_back"):
        back = lax.all_to_all(sent.reshape(NORB, ROWS + 1, 1, LANES), ORB, 0, 0, tiled=True)
    with jax.named_scope("rms"):
        slab = jnp.sum(back[:, ROWS, 0, :], axis=0)
        squares = jnp.sum(copies(slab, COMP), axis=0)[:NORB]
        grad_rms = jnp.sqrt(squares / CELLS)
    with jax.named_scope("unpack"):
        new = call(unpack_kernel, f32(16, NY, NZ), "unpack", 1 << 20, 2 * mib)(back.reshape(NORB * (ROWS + 1), LANES))
    return new[None], grad_rms


def solution(mesh):
    fine = Mesh(mesh.devices.reshape(4, 16, 4, 2), ("x", "z", "y", "core"))
    return jax.shard_map(
        on_device,
        mesh=fine,
        in_specs=(P(ORB, COMP, None, None), P(COMP, None, None), P(None, COMP, None)),
        out_specs=(P(ORB, COMP, None, None), P()),
        check_vma=False,
    )
```

```python
import math

import jax
import jax.numpy as jnp
import numpy as np
from jax import lax
from jax.experimental import pallas as pl
from jax.experimental.pallas import tpu as pltpu
from jax.sharding import Mesh
from jax.sharding import PartitionSpec as P

spacing = 0.4
descent = 0.02
NX, NY, NZ, NORB = 128, 128, 128, 64
CELLS = NX * NY * NZ
KINETIC = -0.5 / spacing**2
REACH = 7
XG, YB, XL, ZB = 4, 8, 4, 32
ROWS, LANES = XG * YB, XL * ZB
HIGH = lax.Precision.HIGHEST
PARAMS = pltpu.CompilerParams(vmem_limit_bytes=12 * 1024 * 1024)
ORB, COMP = ("x", "z"), ("y", "core")


def second_coefs_list():
    terms = []
    for k in range(1, REACH + 1):
        terms.append(
            2.0
            * (-1) ** (k + 1)
            * math.factorial(REACH) ** 2
            / (k * k * math.factorial(REACH - k) * math.factorial(REACH + k))
        )
    return [-2.0 * sum(terms)] + terms


COEFS = [KINETIC * c for c in second_coefs_list()]


def coef(k):
    return COEFS[k] if 1 <= k <= REACH else 0.0


def inner_matrix():
    x, z = 16, ZB
    line_x = np.array([[coef(abs(i - j)) for j in range(x)] for i in range(x)])
    line_z = np.array([[coef(abs(i - j)) for j in range(z)] for i in range(z)])
    return (np.kron(line_x, np.eye(z)) + np.kron(np.eye(x), line_z)).astype(np.float32)


def edge_matrix():
    table = np.zeros((2, 4 * LANES, 4 * LANES))
    for x in range(16):
        for z in range(ZB):
            out = x * ZB + z
            for layer in range(8):
                table[0, layer * ZB + z, out] += coef(x + 8 - layer)
                table[1, layer * ZB + z, out] += coef(16 + layer - x)
            for t in range(8):
                row = 2 * LANES + (x % XL) * ZB + (x // XL) * 8 + t
                table[:, row, out] += coef(ZB + t - z)
                table[:, row + LANES, out] += coef(z + 8 - t)
    return np.concatenate([table[0, :, : 2 * LANES], table[1, :, 2 * LANES :]], axis=1)


def split(value):
    high = value.astype(jnp.bfloat16)
    return high, (value - high.astype(jnp.float32)).astype(jnp.bfloat16)


def three_products(left, right, dims=(((1,), (0,)), ((), ()))):
    def product(a, b):
        return lax.dot_general(a, b, dims, preferred_element_type=jnp.float32)

    return product(left[0], right[0]) + (product(left[1], right[0]) + product(left[0], right[1]))


def pack_kernel(src, dst):
    group = lax.broadcasted_iota(jnp.int32, (32, LANES), 1) // ZB
    for xg in range(XG):
        for part in range(4):
            rows = slice(part * 32, part * 32 + 32)
            layers = [src[xg * XL + x, rows, :] for x in range(XL)]
            for q in range(4):
                piece = layers[q]
                for x in range(XL):
                    if x != q:
                        moved = pltpu.roll(layers[x], ((x - q) * ZB) % LANES, 1)
                        piece = jnp.where(group == x, moved, piece)
                first = q * 16 + part * 4
                dst[first : first + 4, xg * YB : (xg + 1) * YB, :] = piece.reshape(4, YB, LANES)


def unpack_kernel(src, dst):
    group = lax.broadcasted_iota(jnp.int32, (YB, LANES), 1) // ZB
    for yb in range(16):
        for xg in range(XG):
            pieces = [src[pl.ds((q * 16 + yb) * (ROWS + 1) + xg * YB, YB), :] for q in range(4)]
            for x in range(XL):
                layer = pieces[x]
                for q in range(4):
                    if q != x:
                        moved = pltpu.roll(pieces[q], ((q - x) * ZB) % LANES, 1)
                        layer = jnp.where(group == q, moved, layer)
                dst[xg * XL + x, yb * YB : (yb + 1) * YB, :] = layer


def spread_kernel(src, phi, *refs):
    sent, kept, sems = refs[:6], refs[6:12], refs[12]
    y_up, y_down, x_up, x_down, z_up, z_down = kept
    moves = [pltpu.make_async_copy(kept[i], sent[i], sems.at[i]) for i in range(6)]
    slot = (lax.broadcasted_iota(jnp.int32, (NORB, LANES), 1) % ZB) // 8
    for y in range(YB):
        up = down = jnp.zeros((NORB, LANES), jnp.float32)
        for xg in range(XG):
            r = xg * YB + y
            row = src[pl.ds(r, NORB, stride=ROWS), :]
            phi[r] = row
            if y < REACH:
                y_up[xg * REACH + y] = row
            if y >= 1:
                y_down[xg * REACH + y - 1] = row
            if xg < 2:
                x_up[r] = row
            else:
                x_down[r - 2 * YB] = row
            up = jnp.where(slot == xg, pltpu.roll(row, xg * 8, 1) if xg else row, up)
            down = jnp.where(slot == xg, pltpu.roll(row, (xg * 8 - 24) % LANES, 1) if xg != 3 else row, down)
        z_up[y] = up
        z_down[y] = down
        if y == REACH - 1:
            moves[0].start()
    for i in range(1, 6):
        moves[i].start()
    for move in moves:
        move.wait()


def constants_kernel(place, potential, segments, diagonal, inside):
    x_pos, z_pos = place[0], place[1]
    lane = lax.broadcasted_iota(jnp.int32, (YB, LANES), 1)
    first_row = pl.multiple_of(z_pos * YB, YB)
    pick = lax.broadcasted_iota(jnp.int32, (YB, NY), 1) == z_pos * YB + lax.broadcasted_iota(jnp.int32, (YB, NY), 0)
    ends = []
    for side in range(2):
        table = segments[side].astype(jnp.float32)
        ends.append(
            lax.dot_general(
                pick.astype(jnp.float32), table, (((1,), (1,)), ((), ())), precision=HIGH, preferred_element_type=jnp.float32
            )
        )
    depth = (x_pos * ZB + lane % ZB).astype(jnp.float32)
    layer = lax.broadcasted_iota(jnp.int32, (16, LANES), 0)
    for xg in range(XG):
        block = jnp.zeros((YB, LANES), jnp.float32)
        for x in range(XL):
            rows = potential[xg * XL + x, pl.ds(first_row, YB), :]
            moved = pltpu.roll(rows, lax.rem(x * ZB + LANES - x_pos * ZB, LANES), 1)
            block = jnp.where(lane // ZB == x, moved, block)
        diagonal[xg * YB : (xg + 1) * YB, :] = block + jnp.float32(3.0 * COEFS[0])
        widen = layer == xg * XL + lax.broadcasted_iota(jnp.int32, (16, LANES), 1) // ZB
        low, high = (
            jnp.dot(e, widen.astype(jnp.float32), precision=HIGH, preferred_element_type=jnp.float32) for e in ends
        )
        held = jnp.where(depth >= low, 1.0, 0.0) * jnp.where(depth < high, 1.0, 0.0)
        inside[xg * YB : (xg + 1) * YB, :] = held


def tall(ref, xg):
    return ref[xg * YB : (xg + 1) * YB].reshape(YB * NORB, LANES)


def pair_sums(left, right):
    left, right = jnp.concatenate(left, axis=1), jnp.concatenate(right, axis=1)
    return lax.dot_general(
        left, right, (((1,), (1,)), ((), ())), precision=HIGH, preferred_element_type=jnp.float32
    )


def inner_kernel(phi, diagonal, matrix, images, sums):
    total = jnp.zeros((NORB, NORB), jnp.float32)
    for pair in range(2):
        cells = jnp.concatenate([tall(phi, xg) for xg in range(XG)], axis=1)
        columns = slice(pair * 2 * LANES, (pair + 1) * 2 * LANES)
        both = jnp.dot(cells, matrix[:, columns], precision=HIGH, preferred_element_type=jnp.float32)
        for xg in (2 * pair, 2 * pair + 1):
            own = slice((xg % 2) * LANES, (xg % 2 + 1) * LANES)
            rows = [phi[xg * YB + y] for y in range(YB)]
            values = []
            for y in range(YB):
                r = xg * YB + y
                value = both[y * NORB : (y + 1) * NORB, own] + diagonal[r : r + 1, :] * rows[y]
                for other in range(YB):
                    if other != y:
                        value = value + COEFS[abs(other - y)] * rows[other]
                images[r] = value
                values.append(value)
            total = total + pair_sums(rows, values)
    sums[...] = total


def edge_kernel(phi, inner, sums, high, low, *refs):
    came, images, partial, kept, sems = refs[:6], refs[6], refs[7], refs[8:14], refs[14]
    y_up, y_down, x_up, x_down, z_up, z_down = kept
    moves = [pltpu.make_async_copy(came[i], kept[i], sems.at[i]) for i in range(6)]
    for move in moves:
        move.start()
    for move in moves:
        move.wait()
    total = sums[...]
    z_halo = [z_up[...].reshape(YB * NORB, LANES), z_down[...].reshape(YB * NORB, LANES)]
    for pair in range(2):
        x_halo = x_up if pair else x_down
        halo = split(jnp.concatenate([tall(x_halo, 0), tall(x_halo, 1)] + z_halo, axis=1))
        columns = slice(pair * 2 * LANES, (pair + 1) * 2 * LANES)
        both = three_products(halo, (high[:, columns], low[:, columns]))
        for xg in (2 * pair, 2 * pair + 1):
            own = slice((xg % 2) * LANES, (xg % 2 + 1) * LANES)
            above = [y_up[xg * REACH + i] for i in range(REACH)]
            below = [y_down[xg * REACH + i] for i in range(REACH)]
            values = []
            for y in range(YB):
                value = both[y * NORB : (y + 1) * NORB, own]
                for i in range(REACH):
                    if YB + i - y <= REACH:
                        value = value + COEFS[YB + i - y] * above[i]
                    if 1 <= y + REACH - i <= REACH:
                        value = value + COEFS[y + REACH - i] * below[i]
                images[xg * YB + y] = inner[xg * YB + y] + value
                values.append(value)
            left = split(jnp.concatenate([phi[xg * YB + y] for y in range(YB)], axis=1))
            right = split(jnp.concatenate(values, axis=1))
            total = total + three_products(left, right, (((1,), (1,)), ((), ())))
    packed = jnp.concatenate([total[: NORB // 2], total[NORB // 2 :]], axis=1)
    partial[...] = jnp.broadcast_to(packed[None], partial.shape)


def sum_kernel(came, sent):
    sent[...] = jnp.broadcast_to(jnp.sum(came[...], axis=0)[None], sent.shape)


def update_kernel(phi, images, sums, inside, out):
    packed = jnp.sum(sums[...], axis=0)
    half = jnp.concatenate([packed[:, :NORB], packed[:, NORB:]], axis=0)
    lag = (half + half.T) * jnp.float32(0.5 / CELLS)
    squares = jnp.zeros((NORB, LANES), jnp.float32)
    for xg in range(XG):
        rows = [phi[xg * YB + y] for y in range(YB)]
        mixed = jnp.dot(lag, jnp.concatenate(rows, axis=1), precision=HIGH, preferred_element_type=jnp.float32)
        for y in range(YB):
            r = xg * YB + y
            gradient = images[r] - mixed[:, y * LANES : (y + 1) * LANES]
            squares = squares + gradient * gradient
            moved = rows[y] - descent * gradient
            out[pl.ds(r, NORB, stride=ROWS + 1), :] = jnp.where(inside[r : r + 1, :] > 0.0, moved, 0.0)
    ones = jnp.ones((8, LANES), jnp.float32)
    sums = lax.dot_general(ones, squares, (((1,), (1,)), ((), ())), precision=HIGH, preferred_element_type=jnp.float32)
    sums = jnp.concatenate([sums, jnp.zeros((8, LANES - NORB), jnp.float32)], axis=1)
    out[pl.ds(ROWS, NORB, stride=ROWS + 1), :] = jnp.broadcast_to(sums[0:1, :], (NORB, LANES))


def f32(*shape):
    return jax.ShapeDtypeStruct(shape, jnp.float32)


def call(kernel, out_shape, name, flops, nbytes, **more):
    return pl.pallas_call(
        kernel,
        out_shape=out_shape,
        compiler_params=PARAMS,
        name=name,
        cost_estimate=pl.CostEstimate(flops=flops, bytes_accessed=nbytes, transcendentals=0),
        **more,
    )


def exchange(value, axes):
    return lax.all_to_all(value, axes, 0, 0, tiled=True)


def shift(value, axes, count, up):
    pairs = [(i + 1, i) if up else (i, i + 1) for i in range(count - 1)]
    return lax.ppermute(value, axes, pairs)


def on_device(orbitals, potential, segments):
    mib = 1 << 20
    with jax.named_scope("pack"):
        pieces = call(pack_kernel, f32(NORB, ROWS, LANES), "pack", 1 << 20, 2 * mib)(orbitals[0])
    with jax.named_scope("transpose"):
        arrived = lax.all_to_all(pieces, ORB, 0, 0, tiled=True).reshape(NORB * ROWS, LANES)

    with jax.named_scope("block_constants"):
        place = jnp.stack([lax.axis_index("x"), lax.axis_index("z")]).astype(jnp.int32)
        vmem = pl.BlockSpec(memory_space=pltpu.VMEM)
        diagonal, inside = call(
            constants_kernel,
            [f32(ROWS, LANES)] * 2,
            "constants",
            1 << 20,
            mib,
            in_specs=[pl.BlockSpec(memory_space=pltpu.SMEM), vmem, vmem],
        )(place, potential, segments)
    inner, edge = inner_matrix(), edge_matrix()
    edge_high = edge.astype(jnp.bfloat16)
    edge_low = (edge - edge_high.astype(np.float64)).astype(jnp.bfloat16)

    whole = f32(ROWS, NORB, LANES)
    y_side, x_side, z_side = (f32(n, NORB, LANES) for n in (XG * REACH, 2 * YB, YB))
    sides = [y_side, y_side, x_side, x_side, z_side, z_side]
    far = pl.BlockSpec(memory_space=pltpu.HBM)
    slots = [pltpu.VMEM(side.shape, jnp.float32) for side in sides] + [pltpu.SemaphoreType.DMA((6,))]
    with jax.named_scope("spread"):
        phi, *sides = call(
            spread_kernel,
            [whole] + sides,
            "spread",
            1 << 20,
            8 * mib,
            out_specs=[vmem] + [far] * 6,
            scratch_shapes=slots,
        )(arrived)
    y_up, y_down, x_up, x_down, z_up, z_down = sides
    with jax.named_scope("halo"):
        y_up = shift(y_up, "z", 16, True)
        y_down = shift(y_down, "z", 16, False)
        x_up = shift(x_up, COMP, 8, True)
        x_down = shift(x_down, COMP, 8, False)
        z_up = shift(z_up, "x", 4, True)
        z_down = shift(z_down, "x", 4, False)
    with jax.named_scope("inner"):
        images, sums = call(inner_kernel, [whole, f32(NORB, NORB)], "inner", 1 << 32, 2 * mib)(
            phi, diagonal, jnp.asarray(inner)
        )
    with jax.named_scope("edge"):
        images, partial = call(
            edge_kernel,
            [whole, f32(16, NORB // 2, 2 * NORB)],
            "edge",
            1 << 31,
            6 * mib,
            in_specs=[vmem] * 5 + [far] * 6,
            scratch_shapes=slots,
        )(phi, images, sums, jnp.asarray(edge_high), jnp.asarray(edge_low), y_up, y_down, x_up, x_down, z_up, z_down)
    with jax.named_scope("correlation_sum"):
        partial = exchange(partial, ("x", "y"))
        partial = call(sum_kernel, f32(2, NORB // 2, 2 * NORB), "sum_plane", 1 << 16, mib)(partial)
        partial = exchange(partial, ("core",))
        partial = call(sum_kernel, f32(16, NORB // 2, 2 * NORB), "sum_chip", 1 << 16, mib)(partial)
        partial = exchange(partial, ("z",))
    with jax.named_scope("update"):
        sent = call(update_kernel, f32(NORB * (ROWS + 1), LANES), "update", 1 << 28, 3 * mib)(
            phi, images, partial, inside
        )
    with jax.named_scope("transpose_back"):
        back = lax.all_to_all(sent.reshape(NORB, ROWS + 1, 1, LANES), ORB, 0, 0, tiled=True)
    with jax.named_scope("rms"):
        slab = jnp.sum(back[:, ROWS, 0, :], axis=0)
        sent = jnp.broadcast_to(slab, (8, 1, LANES))
        squares = jnp.sum(exchange(sent, COMP), axis=(0, 1))[:NORB]
        grad_rms = jnp.sqrt(squares / CELLS)
    with jax.named_scope("unpack"):
        new = call(unpack_kernel, f32(16, NY, NZ), "unpack", 1 << 20, 2 * mib)(back.reshape(NORB * (ROWS + 1), LANES))
    return new[None], grad_rms


def solution(mesh):
    fine = Mesh(mesh.devices.reshape(4, 16, 4, 2), ("x", "z", "y", "core"))
    return jax.shard_map(
        on_device,
        mesh=fine,
        in_specs=(P(ORB, COMP, None, None), P(COMP, None, None), P(None, COMP, None)),
        out_specs=(P(ORB, COMP, None, None), P()),
        check_vma=False,
    )
```

```python
import functools
import math

import jax
import jax.numpy as jnp
import numpy as np
from jax import lax
from jax.experimental import pallas as pl
from jax.experimental.pallas import tpu as pltpu
from jax.sharding import Mesh
from jax.sharding import PartitionSpec as P

spacing = 0.4
descent = 0.02
NX, NY, NZ, NORB = 128, 128, 128, 64
CELLS = NX * NY * NZ
KINETIC = -0.5 / spacing**2
REACH = 7
XG, YB, XL, ZB = 4, 8, 4, 32
ROWS, LANES = XG * YB, XL * ZB
FOLD, SLOT = 17, 24
HIGH = lax.Precision.HIGHEST
PARAMS = pltpu.CompilerParams(vmem_limit_bytes=12 * 1024 * 1024)
ORB, COMP = ("x", "z"), ("y", "core")


def second_coefs_list():
    terms = []
    for k in range(1, REACH + 1):
        terms.append(
            2.0
            * (-1) ** (k + 1)
            * math.factorial(REACH) ** 2
            / (k * k * math.factorial(REACH - k) * math.factorial(REACH + k))
        )
    return [-2.0 * sum(terms)] + terms


COEFS = [KINETIC * c for c in second_coefs_list()]


def coef(k):
    return COEFS[k] if 1 <= k <= REACH else 0.0


def inner_matrix():
    x, z = 16, ZB
    line_x = np.array([[coef(abs(i - j)) for j in range(x)] for i in range(x)])
    line_z = np.array([[coef(abs(i - j)) for j in range(z)] for i in range(z)])
    return (np.kron(line_x, np.eye(z)) + np.kron(np.eye(x), line_z)).astype(np.float32)


def edge_matrix():
    table = np.zeros((2, 4 * LANES, 4 * LANES))
    for x in range(16):
        for z in range(ZB):
            out = x * ZB + z
            for layer in range(8):
                table[0, layer * ZB + z, out] += coef(x + 8 - layer)
                table[1, layer * ZB + z, out] += coef(16 + layer - x)
            for t in range(8):
                row = 2 * LANES + (x % XL) * ZB + (x // XL) * 8 + t
                table[:, row, out] += coef(ZB + t - z)
                table[:, row + LANES, out] += coef(z + 8 - t)
    return np.concatenate([table[0, :, : 2 * LANES], table[1, :, 2 * LANES :]], axis=1)


def split(value):
    high = value.astype(jnp.bfloat16)
    return high, (value - high.astype(jnp.float32)).astype(jnp.bfloat16)


def three_products(left, right, dims=(((1,), (0,)), ((), ()))):
    def product(a, b):
        return lax.dot_general(a, b, dims, preferred_element_type=jnp.float32)

    return product(left[0], right[0]) + (product(left[1], right[0]) + product(left[0], right[1]))


def pack_kernel(src, dst):
    group = lax.broadcasted_iota(jnp.int32, (32, LANES), 1) // ZB
    for xg in range(XG):
        for part in range(4):
            rows = slice(part * 32, part * 32 + 32)
            layers = [src[xg * XL + x, rows, :] for x in range(XL)]
            for q in range(4):
                piece = layers[q]
                for x in range(XL):
                    if x != q:
                        moved = pltpu.roll(layers[x], ((x - q) * ZB) % LANES, 1)
                        piece = jnp.where(group == x, moved, piece)
                first = q * 16 + part * 4
                dst[first : first + 4, xg * YB : (xg + 1) * YB, :] = piece.reshape(4, YB, LANES)


def unpack_kernel(src, dst):
    group = lax.broadcasted_iota(jnp.int32, (YB, LANES), 1) // ZB
    for yb in range(16):
        for xg in range(XG):
            pieces = [src[pl.ds((q * 16 + yb) * (ROWS + 1) + xg * YB, YB), :] for q in range(4)]
            for x in range(XL):
                layer = pieces[x]
                for q in range(4):
                    if q != x:
                        moved = pltpu.roll(pieces[q], ((q - x) * ZB) % LANES, 1)
                        layer = jnp.where(group == q, moved, layer)
                dst[xg * XL + x, yb * YB : (yb + 1) * YB, :] = layer


def spread_kernel(src, phi, *refs):
    sent, kept, sems = refs[:6], refs[6:12], refs[12]
    y_up, y_down, x_up, x_down, z_up, z_down = kept
    moves = [pltpu.make_async_copy(kept[i], sent[i], sems.at[i]) for i in range(6)]
    slot = (lax.broadcasted_iota(jnp.int32, (NORB, LANES), 1) % ZB) // 8
    for xg in range(XG):
        x_side = x_up if xg < 2 else x_down
        for y in range(YB):
            r = xg * YB + y
            row = src[pl.ds(r, NORB, stride=ROWS), :]
            phi[r] = row
            x_side[xg % 2 * YB + y] = row
            if y < REACH:
                y_up[xg * REACH + y] = row
            if y >= 1:
                y_down[xg * REACH + y - 1] = row
            up = pltpu.roll(row, xg * 8, 1) if xg else row
            down = pltpu.roll(row, (xg * 8 - 24) % LANES, 1) if xg != 3 else row
            z_up[y] = jnp.where(slot == xg, up, z_up[y]) if xg else up
            z_down[y] = jnp.where(slot == xg, down, z_down[y]) if xg else down
        if xg == 1:
            moves[2].start()
    for i in (0, 1, 3, 4, 5):
        moves[i].start()
    for move in moves:
        move.wait()


def constants_kernel(place, potential, segments, diagonal, inside):
    x_pos, z_pos = place[0], place[1]
    lane = lax.broadcasted_iota(jnp.int32, (YB, LANES), 1)
    first_row = pl.multiple_of(z_pos * YB, YB)
    pick = lax.broadcasted_iota(jnp.int32, (YB, NY), 1) == z_pos * YB + lax.broadcasted_iota(jnp.int32, (YB, NY), 0)
    ends = []
    for side in range(2):
        table = segments[side].astype(jnp.float32)
        ends.append(
            lax.dot_general(
                pick.astype(jnp.float32), table, (((1,), (1,)), ((), ())), precision=HIGH, preferred_element_type=jnp.float32
            )
        )
    depth = (x_pos * ZB + lane % ZB).astype(jnp.float32)
    layer = lax.broadcasted_iota(jnp.int32, (16, LANES), 0)
    for xg in range(XG):
        block = jnp.zeros((YB, LANES), jnp.float32)
        for x in range(XL):
            rows = potential[xg * XL + x, pl.ds(first_row, YB), :]
            moved = pltpu.roll(rows, lax.rem(x * ZB + LANES - x_pos * ZB, LANES), 1)
            block = jnp.where(lane // ZB == x, moved, block)
        diagonal[xg * YB : (xg + 1) * YB, :] = block + jnp.float32(3.0 * COEFS[0])
        widen = layer == xg * XL + lax.broadcasted_iota(jnp.int32, (16, LANES), 1) // ZB
        low, high = (
            jnp.dot(e, widen.astype(jnp.float32), precision=HIGH, preferred_element_type=jnp.float32) for e in ends
        )
        held = jnp.where(depth >= low, 1.0, 0.0) * jnp.where(depth < high, 1.0, 0.0)
        inside[xg * YB : (xg + 1) * YB, :] = held


def tall(ref, xg):
    return ref[xg * YB : (xg + 1) * YB].reshape(YB * NORB, LANES)


def pair_sums(left, right):
    left, right = jnp.concatenate(left, axis=1), jnp.concatenate(right, axis=1)
    return lax.dot_general(
        left, right, (((1,), (1,)), ((), ())), precision=HIGH, preferred_element_type=jnp.float32
    )


def inner_kernel(phi, diagonal, matrix, images, sums):
    total = jnp.zeros((NORB, NORB), jnp.float32)
    for pair in range(2):
        cells = jnp.concatenate([tall(phi, xg) for xg in range(XG)], axis=1)
        columns = slice(pair * 2 * LANES, (pair + 1) * 2 * LANES)
        both = jnp.dot(cells, matrix[:, columns], precision=HIGH, preferred_element_type=jnp.float32)
        for xg in (2 * pair, 2 * pair + 1):
            own = slice((xg % 2) * LANES, (xg % 2 + 1) * LANES)
            rows = [phi[xg * YB + y] for y in range(YB)]
            values = []
            for y in range(YB):
                r = xg * YB + y
                value = both[y * NORB : (y + 1) * NORB, own] + diagonal[r : r + 1, :] * rows[y]
                for other in range(YB):
                    if other != y:
                        value = value + COEFS[abs(other - y)] * rows[other]
                images[r] = value
                values.append(value)
            total = total + pair_sums(rows, values)
    sums[...] = total


def fold(table):
    n = NORB // 2
    above = lax.broadcasted_iota(jnp.int32, (n, n), 0) - lax.broadcasted_iota(jnp.int32, (n, n), 1)
    last = table[n:, n:]
    corner = table[:n, n:]
    mixed = jnp.where(above <= 0, table[:n, :n], last)
    diagonal = jnp.sum(jnp.where(above == 0, last, 0.0), axis=0, keepdims=True)
    top = jnp.concatenate([corner[: n // 2], corner[n // 2 :], mixed[: n // 2], mixed[n // 2 :]], axis=1)
    bottom = jnp.concatenate([diagonal, jnp.zeros((1, LANES - n), jnp.float32)], axis=1)
    return top, bottom


def unfold(top, bottom):
    n = NORB // 2
    above = lax.broadcasted_iota(jnp.int32, (n, n), 0) - lax.broadcasted_iota(jnp.int32, (n, n), 1)
    corner = jnp.concatenate([top[:, :n], top[:, n : 2 * n]], axis=0)
    mixed = jnp.concatenate([top[:, 2 * n : 3 * n], top[:, 3 * n :]], axis=0)
    turned = mixed.T
    first = jnp.where(above <= 0, mixed, turned)
    last = jnp.where(above > 0, mixed, jnp.where(above == 0, bottom[:, :n], turned))
    left = jnp.concatenate([first, corner.T], axis=0)
    right = jnp.concatenate([corner, last], axis=0)
    return jnp.concatenate([left, right], axis=1)


def arrive(came, kept, sems):
    moves = [pltpu.make_async_copy(came[i], kept[i], sems.at[i]) for i in range(len(came))]
    for move in moves:
        move.start()
    return moves


def edge_kernel(phi, inner, sums, high, low, *refs):
    came, images, partial, kept, sems = refs[:6], refs[6], refs[7], refs[8:14], refs[14]
    y_up, y_down, x_up, x_down, z_up, z_down = kept
    moves = arrive(came, kept, sems)
    for i in (2, 3, 4, 5, 0, 1):
        moves[i].wait()
    total = sums[...]
    z_halo = [z_up[...].reshape(YB * NORB, LANES), z_down[...].reshape(YB * NORB, LANES)]
    for pair in range(2):
        x_halo = x_up if pair else x_down
        halo = split(jnp.concatenate([tall(x_halo, 0), tall(x_halo, 1)] + z_halo, axis=1))
        columns = slice(pair * 2 * LANES, (pair + 1) * 2 * LANES)
        both = three_products(halo, (high[:, columns], low[:, columns]))
        for xg in (2 * pair, 2 * pair + 1):
            own = slice((xg % 2) * LANES, (xg % 2 + 1) * LANES)
            above = [y_up[xg * REACH + i] for i in range(REACH)]
            below = [y_down[xg * REACH + i] for i in range(REACH)]
            values = []
            for y in range(YB):
                value = both[y * NORB : (y + 1) * NORB, own]
                for i in range(REACH):
                    if YB + i - y <= REACH:
                        value = value + COEFS[YB + i - y] * above[i]
                    if 1 <= y + REACH - i <= REACH:
                        value = value + COEFS[y + REACH - i] * below[i]
                images[xg * YB + y] = inner[xg * YB + y] + value
                values.append(value)
            left = split(jnp.concatenate([phi[xg * YB + y] for y in range(YB)], axis=1))
            right = split(jnp.concatenate(values, axis=1))
            total = total + three_products(left, right, (((1,), (1,)), ((), ())))
    top, bottom = fold(total + total.T)
    rest = jnp.zeros((SLOT - FOLD, LANES), jnp.float32)
    for i in range(2):
        partial[i * SLOT : (i + 1) * SLOT, :] = jnp.concatenate([top, bottom, rest], axis=0)


def added(came, count):
    size = came.shape[0] // count
    top = came[0 : FOLD - 1, :]
    bottom = came[FOLD - 1 : FOLD, :]
    for i in range(1, count):
        top = top + came[i * size : i * size + FOLD - 1, :]
        bottom = bottom + came[i * size + FOLD - 1 : i * size + FOLD, :]
    return top, bottom


def sum_kernel(count, came, sent):
    top, bottom = added(came, count)
    for i in range(sent.shape[0] // FOLD):
        sent[i * FOLD : i * FOLD + FOLD - 1, :] = top
        sent[i * FOLD + FOLD - 1 : (i + 1) * FOLD, :] = bottom


def update_kernel(phi, images, sums, inside, out):
    lag = unfold(*added(sums, 16)) * jnp.float32(0.5 / CELLS)
    squares = jnp.zeros((NORB, LANES), jnp.float32)
    for xg in range(XG):
        rows = [phi[xg * YB + y] for y in range(YB)]
        mixed = jnp.dot(lag, jnp.concatenate(rows, axis=1), precision=HIGH, preferred_element_type=jnp.float32)
        for y in range(YB):
            r = xg * YB + y
            gradient = images[r] - mixed[:, y * LANES : (y + 1) * LANES]
            squares = squares + gradient * gradient
            moved = rows[y] - descent * gradient
            out[pl.ds(r, NORB, stride=ROWS + 1), :] = jnp.where(inside[r : r + 1, :] > 0.0, moved, 0.0)
    ones = jnp.ones((8, LANES), jnp.float32)
    sums = lax.dot_general(ones, squares, (((1,), (1,)), ((), ())), precision=HIGH, preferred_element_type=jnp.float32)
    sums = jnp.concatenate([sums, jnp.zeros((8, LANES - NORB), jnp.float32)], axis=1)
    out[pl.ds(ROWS, NORB, stride=ROWS + 1), :] = jnp.broadcast_to(sums[0:1, :], (NORB, LANES))


def f32(*shape):
    return jax.ShapeDtypeStruct(shape, jnp.float32)


def call(kernel, out_shape, name, flops, nbytes, **more):
    return pl.pallas_call(
        kernel,
        out_shape=out_shape,
        compiler_params=PARAMS,
        name=name,
        cost_estimate=pl.CostEstimate(flops=flops, bytes_accessed=nbytes, transcendentals=0),
        **more,
    )


def exchange(value, axes):
    return lax.all_to_all(value, axes, 0, 0, tiled=True)


def exchange_folded(value, axes):
    shape = value.shape
    return exchange(value.reshape(shape[0] // FOLD, FOLD, 1, LANES), axes).reshape(shape)


def shift(value, axes, count, up):
    pairs = [(i + 1, i) if up else (i, i + 1) for i in range(count - 1)]
    return lax.ppermute(value, axes, pairs)


def on_device(orbitals, potential, segments):
    mib = 1 << 20
    with jax.named_scope("pack"):
        pieces = call(pack_kernel, f32(NORB, ROWS, LANES), "pack", 1 << 20, 2 * mib)(orbitals[0])
    with jax.named_scope("transpose"):
        arrived = lax.all_to_all(pieces, ORB, 0, 0, tiled=True).reshape(NORB * ROWS, LANES)

    with jax.named_scope("block_constants"):
        place = jnp.stack([lax.axis_index("x"), lax.axis_index("z")]).astype(jnp.int32)
        vmem = pl.BlockSpec(memory_space=pltpu.VMEM)
        diagonal, inside = call(
            constants_kernel,
            [f32(ROWS, LANES)] * 2,
            "constants",
            1 << 20,
            mib,
            in_specs=[pl.BlockSpec(memory_space=pltpu.SMEM), vmem, vmem],
        )(place, potential, segments)
    inner, edge = inner_matrix(), edge_matrix()
    edge_high = edge.astype(jnp.bfloat16)
    edge_low = (edge - edge_high.astype(np.float64)).astype(jnp.bfloat16)

    whole = f32(ROWS, NORB, LANES)
    y_side, x_side, z_side = (f32(n, NORB, LANES) for n in (XG * REACH, 2 * YB, YB))
    sides = [y_side, y_side, x_side, x_side, z_side, z_side]
    far = pl.BlockSpec(memory_space=pltpu.HBM)

    def slots(shapes):
        return [pltpu.VMEM(one.shape, jnp.float32) for one in shapes] + [pltpu.SemaphoreType.DMA((len(shapes),))]

    with jax.named_scope("spread"):
        phi, *sides_out = call(
            spread_kernel,
            [whole] + [pltpu.HBM(side.shape, jnp.float32) for side in sides],
            "spread",
            1 << 20,
            8 * mib,
            out_specs=[vmem] + [far] * 6,
            scratch_shapes=slots(sides),
        )(arrived)
    y_up, y_down, x_up, x_down, z_up, z_down = sides_out
    with jax.named_scope("halo"):
        y_up = shift(y_up, "z", 16, True)
        y_down = shift(y_down, "z", 16, False)
        x_up = shift(x_up, COMP, 8, True)
        x_down = shift(x_down, COMP, 8, False)
        z_up = shift(z_up, "x", 4, True)
        z_down = shift(z_down, "x", 4, False)
    with jax.named_scope("inner"):
        images, sums = call(inner_kernel, [whole, f32(NORB, NORB)], "inner", 1 << 32, 2 * mib)(
            phi, diagonal, jnp.asarray(inner)
        )
    with jax.named_scope("edge"):
        images, partial = call(
            edge_kernel,
            [whole, f32(2 * SLOT, LANES)],
            "edge",
            1 << 31,
            6 * mib,
            in_specs=[vmem] * 5 + [far] * 6,
            scratch_shapes=slots(sides),
        )(phi, images, sums, jnp.asarray(edge_high), jnp.asarray(edge_low), y_up, y_down, x_up, x_down, z_up, z_down)
    with jax.named_scope("correlation_sum"):
        partial = exchange(partial.reshape(2, SLOT, LANES), ("core",)).reshape(2 * SLOT, LANES)
        partial = call(functools.partial(sum_kernel, 2), f32(16 * FOLD, LANES), "sum_chip", 1 << 16, mib)(partial)
        partial = exchange_folded(partial, ("x", "y"))
        partial = call(functools.partial(sum_kernel, 16), f32(16 * FOLD, LANES), "sum_plane", 1 << 16, mib)(partial)
        partial = exchange_folded(partial, ("z",))
    with jax.named_scope("update"):
        sent = call(update_kernel, f32(NORB * (ROWS + 1), LANES), "update", 1 << 28, 3 * mib)(
            phi, images, partial, inside
        )
    with jax.named_scope("transpose_back"):
        back = lax.all_to_all(sent.reshape(NORB, ROWS + 1, 1, LANES), ORB, 0, 0, tiled=True)
    with jax.named_scope("rms"):
        slab = jnp.sum(back[:, ROWS, 0, :], axis=0)
        sent = jnp.broadcast_to(slab, (8, 1, LANES))
        squares = jnp.sum(exchange(sent, COMP), axis=(0, 1))[:NORB]
        grad_rms = jnp.sqrt(squares / CELLS)
    with jax.named_scope("unpack"):
        new = call(unpack_kernel, f32(16, NY, NZ), "unpack", 1 << 20, 2 * mib)(back.reshape(NORB * (ROWS + 1), LANES))
    return new[None], grad_rms


def solution(mesh):
    fine = Mesh(mesh.devices.reshape(4, 16, 4, 2), ("x", "z", "y", "core"))
    return jax.shard_map(
        on_device,
        mesh=fine,
        in_specs=(P(ORB, COMP, None, None), P(COMP, None, None), P(None, COMP, None)),
        out_specs=(P(ORB, COMP, None, None), P()),
        check_vma=False,
    )
```

```python
import functools
import math

import jax
import jax.numpy as jnp
import numpy as np
from jax import lax
from jax.experimental import pallas as pl
from jax.experimental.pallas import tpu as pltpu
from jax.sharding import Mesh
from jax.sharding import PartitionSpec as P

spacing = 0.4
descent = 0.02
NX, NY, NZ, NORB = 128, 128, 128, 64
CELLS = NX * NY * NZ
KINETIC = -0.5 / spacing**2
REACH = 7
XG, YB, XL, ZB = 4, 8, 4, 32
ROWS, LANES = XG * YB, XL * ZB
FOLD = 17
HIGH = lax.Precision.HIGHEST
PARAMS = pltpu.CompilerParams(vmem_limit_bytes=12 * 1024 * 1024)
ORB, COMP = ("x", "z"), ("y", "core")


def second_coefs_list():
    terms = []
    for k in range(1, REACH + 1):
        terms.append(
            2.0
            * (-1) ** (k + 1)
            * math.factorial(REACH) ** 2
            / (k * k * math.factorial(REACH - k) * math.factorial(REACH + k))
        )
    return [-2.0 * sum(terms)] + terms


COEFS = [KINETIC * c for c in second_coefs_list()]


def coef(k):
    return COEFS[k] if 1 <= k <= REACH else 0.0


def inner_blocks():
    steps = np.arange(XL)[:, None] - np.arange(XL)[None, :]
    line_z = np.array([[coef(abs(i - j)) for j in range(ZB)] for i in range(ZB)])
    blocks = []
    for shift_by in range(-2, 3):
        line_x = np.array([[coef(abs(int(s) - shift_by * XL)) for s in row] for row in steps])
        blocks.append(np.kron(line_x, np.eye(ZB)) + (np.kron(np.eye(XL), line_z) if shift_by == 0 else 0.0))
    return np.stack(blocks).astype(np.float32)


def edge_matrix():
    table = np.zeros((2, 4 * LANES, 4 * LANES))
    for x in range(16):
        for z in range(ZB):
            out = x * ZB + z
            for layer in range(8):
                table[0, layer * ZB + z, out] += coef(x + 8 - layer)
                table[1, layer * ZB + z, out] += coef(16 + layer - x)
            for t in range(8):
                row = 2 * LANES + (x % XL) * ZB + (x // XL) * 8 + t
                table[:, row, out] += coef(ZB + t - z)
                table[:, row + LANES, out] += coef(z + 8 - t)
    return np.concatenate([table[0, :, : 2 * LANES], table[1, :, 2 * LANES :]], axis=1)


def split(value):
    high = value.astype(jnp.bfloat16)
    return high, (value - high.astype(jnp.float32)).astype(jnp.bfloat16)


def three_products(left, right, dims=(((1,), (0,)), ((), ()))):
    def product(a, b):
        return lax.dot_general(a, b, dims, preferred_element_type=jnp.float32)

    return product(left[0], right[0]) + (product(left[1], right[0]) + product(left[0], right[1]))


def pack_kernel(slab, dst, src, out, sems):
    group = lax.broadcasted_iota(jnp.int32, (32, LANES), 1) // ZB
    comes, goes = [], []
    for xg in range(XG):
        layers, rows = pl.ds(xg * XL, XL), pl.ds(xg * YB, YB)
        comes.append(pltpu.make_async_copy(slab.at[layers], src.at[layers], sems.at[0, xg]))
        goes.append(pltpu.make_async_copy(out.at[:, rows], dst.at[:, rows], sems.at[1, xg]))
        comes[xg].start()
    for xg in range(XG):
        comes[xg].wait()
        for part in range(4):
            rows = slice(part * 32, part * 32 + 32)
            layers = [src[xg * XL + x, rows, :] for x in range(XL)]
            for q in range(4):
                piece = layers[q]
                for x in range(XL):
                    if x != q:
                        moved = pltpu.roll(layers[x], ((x - q) * ZB) % LANES, 1)
                        piece = jnp.where(group == x, moved, piece)
                first = q * 16 + part * 4
                out[first : first + 4, xg * YB : (xg + 1) * YB, :] = piece.reshape(4, YB, LANES)
        goes[xg].start()
    for move in goes:
        move.wait()


def unpack_kernel(src, dst):
    group = lax.broadcasted_iota(jnp.int32, (YB, LANES), 1) // ZB
    for yb in range(16):
        for xg in range(XG):
            pieces = [src[pl.ds((q * 16 + yb) * (ROWS + 1) + xg * YB, YB), :] for q in range(4)]
            for x in range(XL):
                layer = pieces[x]
                for q in range(4):
                    if q != x:
                        moved = pltpu.roll(pieces[q], ((q - x) * ZB) % LANES, 1)
                        layer = jnp.where(group == q, moved, layer)
                dst[xg * XL + x, yb * YB : (yb + 1) * YB, :] = layer


def spread_y_kernel(src, *refs):
    sent, kept, sems = refs[:2], refs[2:4], refs[4]
    moves = []
    for xg in range(XG):
        rows = pl.ds(xg * REACH, REACH)
        for y in range(YB):
            row = src[pl.ds(xg * YB + y, NORB, stride=ROWS), :]
            if y < REACH:
                kept[0][xg * REACH + y] = row
            if y >= 1:
                kept[1][xg * REACH + y - 1] = row
        for side in range(2):
            moves.append(pltpu.make_async_copy(kept[side].at[rows], sent[side].at[rows], sems.at[xg, side]))
            moves[-1].start()
    for move in moves:
        move.wait()


def spread_kernel(src, phi, *refs):
    sent, kept, sems = refs[:4], refs[4:8], refs[8]
    x_up, x_down, z_up, z_down = kept
    moves = [pltpu.make_async_copy(kept[i], sent[i], sems.at[i]) for i in range(4)]
    slot = (lax.broadcasted_iota(jnp.int32, (NORB, LANES), 1) % ZB) // 8
    for xg in range(XG):
        x_side = x_up if xg < 2 else x_down
        for y in range(YB):
            r = xg * YB + y
            row = src[pl.ds(r, NORB, stride=ROWS), :]
            phi[r] = row
            x_side[xg % 2 * YB + y] = row
            up = pltpu.roll(row, xg * 8, 1) if xg else row
            down = pltpu.roll(row, (xg * 8 - 24) % LANES, 1) if xg != 3 else row
            z_up[y] = jnp.where(slot == xg, up, z_up[y]) if xg else up
            z_down[y] = jnp.where(slot == xg, down, z_down[y]) if xg else down
        if xg == 1:
            moves[0].start()
    for move in moves[1:]:
        move.start()
    for move in moves:
        move.wait()


def constants_kernel(place, potential, segments, diagonal, inside):
    x_pos, z_pos = place[0], place[1]
    lane = lax.broadcasted_iota(jnp.int32, (YB, LANES), 1)
    first_row = pl.multiple_of(z_pos * YB, YB)
    pick = lax.broadcasted_iota(jnp.int32, (YB, NY), 1) == z_pos * YB + lax.broadcasted_iota(jnp.int32, (YB, NY), 0)
    ends = []
    for side in range(2):
        table = segments[side].astype(jnp.float32)
        ends.append(
            lax.dot_general(
                pick.astype(jnp.float32), table, (((1,), (1,)), ((), ())), precision=HIGH, preferred_element_type=jnp.float32
            )
        )
    depth = (x_pos * ZB + lane % ZB).astype(jnp.float32)
    layer = lax.broadcasted_iota(jnp.int32, (16, LANES), 0)
    for xg in range(XG):
        block = jnp.zeros((YB, LANES), jnp.float32)
        for x in range(XL):
            rows = potential[xg * XL + x, pl.ds(first_row, YB), :]
            moved = pltpu.roll(rows, lax.rem(x * ZB + LANES - x_pos * ZB, LANES), 1)
            block = jnp.where(lane // ZB == x, moved, block)
        diagonal[xg * YB : (xg + 1) * YB, :] = block + jnp.float32(3.0 * COEFS[0])
        widen = layer == xg * XL + lax.broadcasted_iota(jnp.int32, (16, LANES), 1) // ZB
        low, high = (
            jnp.dot(e, widen.astype(jnp.float32), precision=HIGH, preferred_element_type=jnp.float32) for e in ends
        )
        held = jnp.where(depth >= low, 1.0, 0.0) * jnp.where(depth < high, 1.0, 0.0)
        inside[xg * YB : (xg + 1) * YB, :] = held


def tall(ref, xg):
    return ref[xg * YB : (xg + 1) * YB].reshape(YB * NORB, LANES)


def inner_kernel(phi, diagonal, blocks, images, sums):
    total = jnp.zeros((NORB, NORB), jnp.float32)
    nothing = jnp.zeros((LANES, LANES), jnp.float32)
    for pair in range(2):
        matrix = jnp.concatenate(
            [
                jnp.concatenate([blocks[to - xg + 2] if abs(to - xg) <= 2 else nothing for xg in range(XG)], axis=0)
                for to in (2 * pair, 2 * pair + 1)
            ],
            axis=1,
        )
        cells = jnp.concatenate([tall(phi, xg) for xg in range(XG)], axis=1)
        both = jnp.dot(cells, matrix, precision=HIGH, preferred_element_type=jnp.float32)
        for xg in (2 * pair, 2 * pair + 1):
            own = slice((xg % 2) * LANES, (xg % 2 + 1) * LANES)
            rows = [phi[xg * YB + y] for y in range(YB)]
            values = []
            for y in range(YB):
                r = xg * YB + y
                value = both[y * NORB : (y + 1) * NORB, own] + diagonal[r : r + 1, :] * rows[y]
                for other in range(YB):
                    if other != y:
                        value = value + COEFS[abs(other - y)] * rows[other]
                images[r] = value
                values.append(value)
            left, right = split(jnp.concatenate(rows, axis=1)), split(jnp.concatenate(values, axis=1))
            total = total + three_products(left, right, (((1,), (1,)), ((), ())))
    sums[...] = total


def fold(table):
    n = NORB // 2
    above = lax.broadcasted_iota(jnp.int32, (n, n), 0) - lax.broadcasted_iota(jnp.int32, (n, n), 1)
    last = table[n:, n:]
    corner = table[:n, n:]
    mixed = jnp.where(above <= 0, table[:n, :n], last)
    diagonal = jnp.sum(jnp.where(above == 0, last, 0.0), axis=0, keepdims=True)
    top = jnp.concatenate([corner[: n // 2], corner[n // 2 :], mixed[: n // 2], mixed[n // 2 :]], axis=1)
    bottom = jnp.concatenate([diagonal, jnp.zeros((1, LANES - n), jnp.float32)], axis=1)
    return top, bottom


def unfold(top, bottom):
    n = NORB // 2
    above = lax.broadcasted_iota(jnp.int32, (n, n), 0) - lax.broadcasted_iota(jnp.int32, (n, n), 1)
    corner = jnp.concatenate([top[:, :n], top[:, n : 2 * n]], axis=0)
    mixed = jnp.concatenate([top[:, 2 * n : 3 * n], top[:, 3 * n :]], axis=0)
    turned = mixed.T
    first = jnp.where(above <= 0, mixed, turned)
    last = jnp.where(above > 0, mixed, jnp.where(above == 0, bottom[:, :n], turned))
    left = jnp.concatenate([first, corner.T], axis=0)
    right = jnp.concatenate([corner, last], axis=0)
    return jnp.concatenate([left, right], axis=1)


def edge_kernel(phi, inner, sums, high, low, *refs):
    y_up, y_down, x_up, x_down, z_up, z_down, images, partial = refs
    total = sums[...]
    z_halo = [z_up[...].reshape(YB * NORB, LANES), z_down[...].reshape(YB * NORB, LANES)]
    for pair in range(2):
        x_halo = x_up if pair else x_down
        halo = split(jnp.concatenate([tall(x_halo, 0), tall(x_halo, 1)] + z_halo, axis=1))
        columns = slice(pair * 2 * LANES, (pair + 1) * 2 * LANES)
        both = three_products(halo, (high[:, columns], low[:, columns]))
        for xg in (2 * pair, 2 * pair + 1):
            own = slice((xg % 2) * LANES, (xg % 2 + 1) * LANES)
            above = [y_up[xg * REACH + i] for i in range(REACH)]
            below = [y_down[xg * REACH + i] for i in range(REACH)]
            values = []
            for y in range(YB):
                value = both[y * NORB : (y + 1) * NORB, own]
                for i in range(REACH):
                    if YB + i - y <= REACH:
                        value = value + COEFS[YB + i - y] * above[i]
                    if 1 <= y + REACH - i <= REACH:
                        value = value + COEFS[y + REACH - i] * below[i]
                images[xg * YB + y] = inner[xg * YB + y] + value
                values.append(value)
            left = split(jnp.concatenate([phi[xg * YB + y] for y in range(YB)], axis=1))
            right = split(jnp.concatenate(values, axis=1))
            total = total + three_products(left, right, (((1,), (1,)), ((), ())))
    top, bottom = fold(total + total.T)
    store_copies(partial, top, bottom)


def store_copies(sent, top, bottom):
    for i in range(sent.shape[0] // FOLD):
        sent[i * FOLD : i * FOLD + FOLD - 1, :] = top
        sent[i * FOLD + FOLD - 1 : (i + 1) * FOLD, :] = bottom


def added(came, count):
    size = came.shape[0] // count
    top = came[0 : FOLD - 1, :]
    bottom = came[FOLD - 1 : FOLD, :]
    for i in range(1, count):
        top = top + came[i * size : i * size + FOLD - 1, :]
        bottom = bottom + came[i * size + FOLD - 1 : i * size + FOLD, :]
    return top, bottom


def sum_kernel(count, came, sent):
    store_copies(sent, *added(came, count))


def update_kernel(phi, images, sums, inside, out):
    lag = unfold(*added(sums, 32)) * jnp.float32(0.5 / CELLS)
    squares = jnp.zeros((NORB, LANES), jnp.float32)
    for xg in range(XG):
        rows = [phi[xg * YB + y] for y in range(YB)]
        mixed = jnp.dot(lag, jnp.concatenate(rows, axis=1), precision=HIGH, preferred_element_type=jnp.float32)
        for y in range(YB):
            r = xg * YB + y
            gradient = images[r] - mixed[:, y * LANES : (y + 1) * LANES]
            squares = squares + gradient * gradient
            moved = rows[y] - descent * gradient
            out[pl.ds(r, NORB, stride=ROWS + 1), :] = jnp.where(inside[r : r + 1, :] > 0.0, moved, 0.0)
    ones = jnp.ones((8, LANES), jnp.float32)
    sums = lax.dot_general(ones, squares, (((1,), (1,)), ((), ())), precision=HIGH, preferred_element_type=jnp.float32)
    sums = jnp.concatenate([sums, jnp.zeros((8, LANES - NORB), jnp.float32)], axis=1)
    out[pl.ds(ROWS, NORB, stride=ROWS + 1), :] = jnp.broadcast_to(sums[0:1, :], (NORB, LANES))


def squares_kernel(src, sent):
    rows = src[pl.ds(ROWS, NORB, stride=ROWS + 1), :]
    sent[...] = jnp.broadcast_to(jnp.sum(rows, axis=0, keepdims=True), sent.shape)


def f32(*shape):
    return jax.ShapeDtypeStruct(shape, jnp.float32)


def call(kernel, out_shape, name, flops, nbytes, **more):
    return pl.pallas_call(
        kernel,
        out_shape=out_shape,
        compiler_params=PARAMS,
        name=name,
        cost_estimate=pl.CostEstimate(flops=flops, bytes_accessed=nbytes, transcendentals=0),
        **more,
    )


def exchange(value, axes):
    return lax.all_to_all(value, axes, 0, 0, tiled=True)


def exchange_folded(value, axes):
    shape = value.shape
    return exchange(value.reshape(shape[0] // FOLD, FOLD, 1, LANES), axes).reshape(shape)


def shift(value, axes, count, up):
    pairs = [(i + 1, i) if up else (i, i + 1) for i in range(count - 1)]
    return lax.ppermute(value, axes, pairs)


def on_device(orbitals, potential, segments):
    mib = 1 << 20
    far, vmem = pl.BlockSpec(memory_space=pltpu.HBM), pl.BlockSpec(memory_space=pltpu.VMEM)
    with jax.named_scope("pack"):
        pieces = call(
            pack_kernel,
            pltpu.HBM((NORB, ROWS, LANES), jnp.float32),
            "pack",
            1 << 20,
            2 * mib,
            in_specs=[far],
            out_specs=far,
            scratch_shapes=[
                pltpu.VMEM((16, NY, NZ), jnp.float32),
                pltpu.VMEM((NORB, ROWS, LANES), jnp.float32),
                pltpu.SemaphoreType.DMA((2, XG)),
            ],
        )(pltpu.with_memory_space_constraint(orbitals[0], pltpu.HBM))
    with jax.named_scope("transpose"):
        arrived = lax.all_to_all(pieces, ORB, 0, 0, tiled=True).reshape(NORB * ROWS, LANES)

    with jax.named_scope("block_constants"):
        place = jnp.stack([lax.axis_index("x"), lax.axis_index("z")]).astype(jnp.int32)
        diagonal, inside = call(
            constants_kernel,
            [f32(ROWS, LANES)] * 2,
            "constants",
            1 << 20,
            mib,
            in_specs=[pl.BlockSpec(memory_space=pltpu.SMEM), vmem, vmem],
        )(place, potential, segments)
        arrived, diagonal, inside = lax.optimization_barrier((arrived, diagonal, inside))
    inner, edge = inner_blocks(), edge_matrix()
    edge_high = edge.astype(jnp.bfloat16)
    edge_low = (edge - edge_high.astype(np.float64)).astype(jnp.bfloat16)

    whole = f32(ROWS, NORB, LANES)
    y_side, x_side, z_side = (f32(n, NORB, LANES) for n in (XG * REACH, 2 * YB, YB))
    sides = [y_side, y_side, x_side, x_side, z_side, z_side]

    def slots(shapes):
        return [pltpu.VMEM(one.shape, jnp.float32) for one in shapes] + [pltpu.SemaphoreType.DMA((len(shapes),))]

    with jax.named_scope("spread"):
        y_up, y_down = call(
            spread_y_kernel,
            [pltpu.HBM(y_side.shape, jnp.float32)] * 2,
            "spread_y",
            1 << 20,
            3 * mib,
            out_specs=[far] * 2,
            scratch_shapes=[pltpu.VMEM(y_side.shape, jnp.float32)] * 2 + [pltpu.SemaphoreType.DMA((XG, 2))],
        )(arrived)
        phi, x_up, x_down, z_up, z_down = call(
            spread_kernel,
            [whole] + [pltpu.HBM(side.shape, jnp.float32) for side in sides[2:]],
            "spread",
            1 << 20,
            6 * mib,
            out_specs=[vmem] + [far] * 4,
            scratch_shapes=slots(sides[2:]),
        )(arrived)
    with jax.named_scope("halo"):
        y_up = shift(y_up, "z", 16, True)
        y_down = shift(y_down, "z", 16, False)
        x_up = shift(x_up, COMP, 8, True)
        x_down = shift(x_down, COMP, 8, False)
        z_up = shift(z_up, "x", 4, True)
        z_down = shift(z_down, "x", 4, False)
    with jax.named_scope("inner"):
        images, sums = call(inner_kernel, [whole, f32(NORB, NORB)], "inner", 1 << 32, 2 * mib)(
            phi, diagonal, jnp.asarray(inner)
        )
    with jax.named_scope("edge"):
        images, partial = call(
            edge_kernel,
            [whole, f32(16 * FOLD, LANES)],
            "edge",
            1 << 31,
            6 * mib,
        )(phi, images, sums, jnp.asarray(edge_high), jnp.asarray(edge_low), y_up, y_down, x_up, x_down, z_up, z_down)
    with jax.named_scope("correlation_sum"):
        partial = exchange_folded(partial, ("z",))
        partial = call(functools.partial(sum_kernel, 16), f32(32 * FOLD, LANES), "sum_column", 1 << 16, mib)(partial)
        partial = exchange_folded(partial, ("core", "x", "y"))
    with jax.named_scope("update"):
        sent = call(update_kernel, f32(NORB * (ROWS + 1), LANES), "update", 1 << 28, 3 * mib)(
            phi, images, partial, inside
        )
    with jax.named_scope("transpose_back"):
        back = exchange(sent.reshape(NORB, ROWS + 1, 1, LANES), ORB).reshape(NORB * (ROWS + 1), LANES)
    with jax.named_scope("rms"):
        sent = call(squares_kernel, f32(8, LANES), "squares", 1 << 14, 1 << 15)(back)
        squares = jnp.sum(exchange(sent.reshape(8, 1, LANES), COMP), axis=(0, 1))[:NORB]
        grad_rms = jnp.sqrt(squares / CELLS)
    with jax.named_scope("unpack"):
        new = call(unpack_kernel, f32(16, NY, NZ), "unpack", 1 << 20, 2 * mib)(back)
    return new[None], grad_rms


def solution(mesh):
    fine = Mesh(mesh.devices.reshape(4, 16, 4, 2), ("x", "z", "y", "core"))
    return jax.shard_map(
        on_device,
        mesh=fine,
        in_specs=(P(ORB, COMP, None, None), P(COMP, None, None), P(None, COMP, None)),
        out_specs=(P(ORB, COMP, None, None), P()),
        check_vma=False,
    )
```

```python
import functools
import math

import jax
import jax.numpy as jnp
import numpy as np
from jax import lax
from jax.experimental import pallas as pl
from jax.experimental.pallas import tpu as pltpu
from jax.sharding import Mesh
from jax.sharding import PartitionSpec as P

spacing = 0.4
descent = 0.02
NX, NY, NZ, NORB = 128, 128, 128, 64
CELLS = NX * NY * NZ
KINETIC = -0.5 / spacing**2
REACH = 7
XG, YB, XL, ZB = 4, 8, 4, 32
ROWS, LANES = XG * YB, XL * ZB
FOLD = 17
HIGH = lax.Precision.HIGHEST
PARAMS = pltpu.CompilerParams(vmem_limit_bytes=12 * 1024 * 1024)
ORB, COMP = ("x", "z"), ("y", "core")


def second_coefs_list():
    terms = []
    for k in range(1, REACH + 1):
        terms.append(
            2.0
            * (-1) ** (k + 1)
            * math.factorial(REACH) ** 2
            / (k * k * math.factorial(REACH - k) * math.factorial(REACH + k))
        )
    return [-2.0 * sum(terms)] + terms


COEFS = [KINETIC * c for c in second_coefs_list()]


def coef(k):
    return COEFS[k] if 1 <= k <= REACH else 0.0


def inner_blocks():
    steps = np.arange(XL)[:, None] - np.arange(XL)[None, :]
    line_z = np.array([[coef(abs(i - j)) for j in range(ZB)] for i in range(ZB)])
    blocks = []
    for shift_by in range(-2, 3):
        line_x = np.array([[coef(abs(int(s) - shift_by * XL)) for s in row] for row in steps])
        blocks.append(np.kron(line_x, np.eye(ZB)) + (np.kron(np.eye(XL), line_z) if shift_by == 0 else 0.0))
    return np.stack(blocks).astype(np.float32)


def edge_matrix():
    table = np.zeros((3 * LANES, XG * LANES))
    for x in range(16):
        for z in range(ZB):
            out = x * ZB + z
            for layer in range(8):
                table[layer * ZB + z, out] += coef(16 + layer - x)
            for t in range(8):
                table[2 * LANES + (x % XL) * ZB + (x // XL) * 8 + t, out] += coef(ZB + t - z)
    return table


def line_matrix():
    return np.array([[coef(abs(i - j)) for j in range(NZ)] for i in range(NZ)], np.float32)


def split(value):
    high = value.astype(jnp.bfloat16)
    return high, (value - high.astype(jnp.float32)).astype(jnp.bfloat16)


def three_products(left, right, dims=(((1,), (0,)), ((), ()))):
    def product(a, b):
        return lax.dot_general(a, b, dims, preferred_element_type=jnp.float32)

    return product(left[0], right[0]) + (product(left[1], right[0]) + product(left[0], right[1]))


def pack_kernel(slab, dst, src, out, sems):
    group = lax.broadcasted_iota(jnp.int32, (32, LANES), 1) // ZB
    comes, goes = [], []
    for xg in range(XG):
        layers, rows = pl.ds(xg * XL, XL), pl.ds(xg * YB, YB)
        comes.append(pltpu.make_async_copy(slab.at[layers], src.at[layers], sems.at[0, xg]))
        goes.append(pltpu.make_async_copy(out.at[:, rows], dst.at[:, rows], sems.at[1, xg]))
        comes[xg].start()
    for xg in range(XG):
        comes[xg].wait()
        for part in range(4):
            rows = slice(part * 32, part * 32 + 32)
            layers = [src[xg * XL + x, rows, :] for x in range(XL)]
            for q in range(4):
                piece = layers[q]
                for x in range(XL):
                    if x != q:
                        moved = pltpu.roll(layers[x], ((x - q) * ZB) % LANES, 1)
                        piece = jnp.where(group == x, moved, piece)
                first = q * 16 + part * 4
                out[first : first + 4, xg * YB : (xg + 1) * YB, :] = piece.reshape(4, YB, LANES)
        goes[xg].start()
    for move in goes:
        move.wait()


def finish_kernel(src, slab, images, inside, dst, squares, own, sems):
    group = lax.broadcasted_iota(jnp.int32, (YB, LANES), 1) // ZB
    total = jnp.zeros((YB, LANES), jnp.float32)
    moves = []
    for xg in range(XG):
        layers = pl.ds(xg * XL, XL)
        moves.append(pltpu.make_async_copy(images.at[layers], own.at[layers], sems.at[xg]))
        moves[xg].start()
    for xg in range(XG):
        moves[xg].wait()
        for yb in range(16):
            rows = slice(yb * YB, (yb + 1) * YB)
            pieces = [src[pl.ds((q * 16 + yb) * (ROWS + 1) + xg * YB, YB), :] for q in range(4)]
            for x in range(XL):
                mixed = pieces[x]
                for q in range(4):
                    if q != x:
                        moved = pltpu.roll(pieces[q], ((q - x) * ZB) % LANES, 1)
                        mixed = jnp.where(group == q, moved, mixed)
                layer = xg * XL + x
                gradient = own[layer, rows, :] - mixed
                total = total + gradient * gradient
                moved = slab[layer, rows, :] - descent * gradient
                dst[layer, rows, :] = jnp.where(inside[layer, rows, :] > 0.0, moved, 0.0)
    squares[...] = jnp.broadcast_to(jnp.sum(total, keepdims=True), squares.shape)


def owner_kernel(slab, below, above, potential, line, own, squares):
    total = jnp.zeros((NY, NZ), jnp.float32)
    for layer in range(16):
        here = slab[layer]
        value = (potential[layer] + jnp.float32(3.0 * COEFS[0])) * here
        value = value + jnp.dot(line[...], here, precision=HIGH, preferred_element_type=jnp.float32)
        value = value + jnp.dot(here, line[...], precision=HIGH, preferred_element_type=jnp.float32)
        for k in range(1, REACH + 1):
            up, down = layer + k, layer - k
            pair = (slab[up] if up < 16 else above[up - 16]) + (slab[down] if down >= 0 else below[down + REACH])
            value = value + COEFS[k] * pair
        own[layer] = value
        total = total + value * value
    squares[...] = jnp.broadcast_to(jnp.sum(total, keepdims=True), squares.shape)


def spread_y_kernel(src, ready, *refs):
    sent, kept, sems = refs[:2], refs[2:4], refs[4]
    ready[...] = jnp.zeros(ready.shape, jnp.float32)
    moves = [pltpu.make_async_copy(kept[side], sent[side], sems.at[side]) for side in range(2)]
    for xg in range(XG):
        for i in range(REACH):
            y = i if xg < 2 else i + 1
            kept[xg // 2][(xg % 2) * REACH + i] = src[pl.ds(xg * YB + y, NORB, stride=ROWS), :]
        if xg % 2:
            moves[xg // 2].start()
    for move in moves:
        move.wait()


def spread_kernel(src, ready, phi, *refs):
    sent, kept, sems = refs[:2], refs[2:4], refs[4]
    x_up, z_up = kept
    moves = [pltpu.make_async_copy(kept[i], sent[i], sems.at[i]) for i in range(2)]
    lane = lax.broadcasted_iota(jnp.int32, (NORB, LANES), 1)
    slot = (lane % ZB) // 8
    for xg in range(XG):
        for y in range(YB):
            r = xg * YB + y
            row = src[pl.ds(r, NORB, stride=ROWS), :]
            phi[r] = row
            if xg == 0:
                x_up[r] = row
            up = pltpu.roll(row, xg * 8, 1) if xg else row
            z_up[y] = jnp.where(slot == xg, up, z_up[y]) if xg else up
        if xg == 1:
            for y in range(6):
                moved = pltpu.roll(phi[YB + 6 + y // 3], (XL - 1 - y % 3) * ZB, 1)
                x_up[YB + y] = jnp.where(lane >= (XL - 1) * ZB, moved, phi[YB + y])
            moves[0].start()
    moves[1].start()
    for move in moves:
        move.wait()


def constants_kernel(place, potential, diagonal):
    x_pos, z_pos = place[0], place[1]
    lane = lax.broadcasted_iota(jnp.int32, (YB, LANES), 1)
    first_row = pl.multiple_of(z_pos * YB, YB)
    for xg in range(XG):
        block = jnp.zeros((YB, LANES), jnp.float32)
        for x in range(XL):
            rows = potential[xg * XL + x, pl.ds(first_row, YB), :]
            moved = pltpu.roll(rows, lax.rem(x * ZB + LANES - x_pos * ZB, LANES), 1)
            block = jnp.where(lane // ZB == x, moved, block)
        diagonal[xg * YB : (xg + 1) * YB, :] = block + jnp.float32(3.0 * COEFS[0])


def tall(ref, xg):
    return ref[xg * YB : (xg + 1) * YB].reshape(YB * NORB, LANES)


def inner_kernel(phi, diagonal, blocks, sums):
    total = jnp.zeros((NORB, NORB), jnp.float32)
    nothing = jnp.zeros((LANES, LANES), jnp.float32)
    for pair in range(2):
        matrix = jnp.concatenate(
            [
                jnp.concatenate([blocks[to - xg + 2] if abs(to - xg) <= 2 else nothing for xg in range(XG)], axis=0)
                for to in (2 * pair, 2 * pair + 1)
            ],
            axis=1,
        )
        cells = jnp.concatenate([tall(phi, xg) for xg in range(XG)], axis=1)
        both = jnp.dot(cells, matrix, precision=HIGH, preferred_element_type=jnp.float32)
        for xg in (2 * pair, 2 * pair + 1):
            own = slice((xg % 2) * LANES, (xg % 2 + 1) * LANES)
            rows = [phi[xg * YB + y] for y in range(YB)]
            values = []
            for y in range(YB):
                r = xg * YB + y
                value = both[y * NORB : (y + 1) * NORB, own] + diagonal[r : r + 1, :] * rows[y]
                for other in range(YB):
                    if other != y:
                        value = value + COEFS[abs(other - y)] * rows[other]
                values.append(value)
            total = total + lax.dot_general(
                jnp.concatenate(rows, axis=1),
                jnp.concatenate(values, axis=1),
                (((1,), (1,)), ((), ())),
                precision=HIGH,
                preferred_element_type=jnp.float32,
            )
    sums[...] = total


def fold(table):
    n = NORB // 2
    above = lax.broadcasted_iota(jnp.int32, (n, n), 0) - lax.broadcasted_iota(jnp.int32, (n, n), 1)
    last = table[n:, n:]
    corner = table[:n, n:]
    mixed = jnp.where(above <= 0, table[:n, :n], last)
    diagonal = jnp.sum(jnp.where(above == 0, last, 0.0), axis=0, keepdims=True)
    top = jnp.concatenate([corner[: n // 2], corner[n // 2 :], mixed[: n // 2], mixed[n // 2 :]], axis=1)
    bottom = jnp.concatenate([diagonal, jnp.zeros((1, LANES - n), jnp.float32)], axis=1)
    return top, bottom


def unfold(top, bottom):
    n = NORB // 2
    above = lax.broadcasted_iota(jnp.int32, (n, n), 0) - lax.broadcasted_iota(jnp.int32, (n, n), 1)
    corner = jnp.concatenate([top[:, :n], top[:, n : 2 * n]], axis=0)
    mixed = jnp.concatenate([top[:, 2 * n : 3 * n], top[:, 3 * n :]], axis=0)
    turned = mixed.T
    first = jnp.where(above <= 0, mixed, turned)
    last = jnp.where(above > 0, mixed, jnp.where(above == 0, bottom[:, :n], turned))
    left = jnp.concatenate([first, corner.T], axis=0)
    right = jnp.concatenate([corner, last], axis=0)
    return jnp.concatenate([left, right], axis=1)


def edge_kernel(phi, sums, high, low, y_a, y_b, x_up, z_up, partial):
    total = sums[...]
    z_halo = z_up[...].reshape(YB * NORB, LANES)
    place = lax.broadcasted_iota(jnp.int32, (NORB, LANES), 1) // ZB
    next_rows = [x_up[YB + y] for y in range(6)]
    for y in (0, 3):
        parts = [pltpu.roll(next_rows[y + i], (i + 1) * ZB, 1) for i in range(3)]
        next_rows.append(jnp.where(place == 0, parts[0], jnp.where(place == 1, parts[1], parts[2])))
    next_group = jnp.stack(next_rows).reshape(YB * NORB, LANES)
    for pair in range(2):
        parts = [tall(x_up, 0), next_group, z_halo] if pair else [z_halo]
        halo = split(jnp.concatenate(parts, axis=1))
        used = slice(0 if pair else 2 * LANES, 3 * LANES), slice(pair * 2 * LANES, (pair + 1) * 2 * LANES)
        both = three_products(halo, (high[used], low[used]))
        y_halo = y_b if pair else y_a
        for xg in (2 * pair, 2 * pair + 1):
            own = slice((xg % 2) * LANES, (xg % 2 + 1) * LANES)
            rows = [y_halo[(xg % 2) * REACH + i] for i in range(REACH)]
            values = []
            for y in range(YB):
                value = both[y * NORB : (y + 1) * NORB, own]
                for i in range(REACH):
                    k = y + REACH - i if pair else YB + i - y
                    if 1 <= k <= REACH:
                        value = value + COEFS[k] * rows[i]
                values.append(value)
            left = split(jnp.concatenate([phi[xg * YB + y] for y in range(YB)], axis=1))
            right = split(jnp.concatenate(values, axis=1))
            total = total + 2.0 * three_products(left, right, (((1,), (1,)), ((), ())))
    top, bottom = fold(total + total.T)
    store_copies(partial, top, bottom)


def store_copies(sent, top, bottom):
    for i in range(sent.shape[0] // FOLD):
        sent[i * FOLD : i * FOLD + FOLD - 1, :] = top
        sent[i * FOLD + FOLD - 1 : (i + 1) * FOLD, :] = bottom


def added(came, count):
    size = came.shape[0] // count
    top = came[0 : FOLD - 1, :]
    bottom = came[FOLD - 1 : FOLD, :]
    for i in range(1, count):
        top = top + came[i * size : i * size + FOLD - 1, :]
        bottom = bottom + came[i * size + FOLD - 1 : i * size + FOLD, :]
    return top, bottom


def sum_kernel(count, came, sent):
    store_copies(sent, *added(came, count))


def mix_kernel(phi, sums, place, own_squares, out, cross):
    lag = unfold(*added(sums, 32)) * jnp.float32(0.5 / CELLS)
    squares = jnp.zeros((NORB, LANES), jnp.float32)
    for xg in range(XG):
        rows = [phi[xg * YB + y] for y in range(YB)]
        mixed = jnp.dot(lag, jnp.concatenate(rows, axis=1), precision=HIGH, preferred_element_type=jnp.float32)
        for y in range(YB):
            value = mixed[:, y * LANES : (y + 1) * LANES]
            squares = squares + value * value
            out[pl.ds(xg * YB + y, NORB, stride=ROWS + 1), :] = value
    across = (((1,), (1,)), ((), ()))
    ones = jnp.ones((8, LANES), jnp.float32)
    sums_row = lax.dot_general(ones, squares, across, precision=HIGH, preferred_element_type=jnp.float32)
    products = lax.dot_general(ones[:, :NORB], lag * lag, across, precision=HIGH, preferred_element_type=jnp.float32)
    lane = lax.broadcasted_iota(jnp.int32, (8, NORB), 1)
    images = jnp.where(lane == place[0] * 16 + place[1], own_squares[:, :NORB], 0.0)
    row = jnp.concatenate([sums_row, images], axis=1)
    out[pl.ds(ROWS, NORB, stride=ROWS + 1), :] = jnp.broadcast_to(row[0:1, :], (NORB, LANES))
    cross[...] = jnp.concatenate([products * jnp.float32(CELLS), jnp.zeros((8, LANES - NORB), jnp.float32)], axis=1)


def squares_kernel(src, sent):
    rows = src[pl.ds(ROWS, NORB, stride=ROWS + 1), :]
    sent[...] = jnp.broadcast_to(jnp.sum(rows, axis=0, keepdims=True), sent.shape)


def f32(*shape):
    return jax.ShapeDtypeStruct(shape, jnp.float32)


def call(kernel, out_shape, name, flops, nbytes, **more):
    return pl.pallas_call(
        kernel,
        out_shape=out_shape,
        compiler_params=PARAMS,
        name=name,
        cost_estimate=pl.CostEstimate(flops=flops, bytes_accessed=nbytes, transcendentals=0),
        **more,
    )


def exchange(value, axes):
    return lax.all_to_all(value, axes, 0, 0, tiled=True)


def exchange_folded(value, axes):
    shape = value.shape
    return exchange(value.reshape(shape[0] // FOLD, FOLD, 1, LANES), axes).reshape(shape)


def shift(value, axes, count, up):
    pairs = [(i + 1, i) if up else (i, i + 1) for i in range(count - 1)]
    return lax.ppermute(value, axes, pairs)


def on_device(orbitals, potential, segments):
    mib = 1 << 20
    far, vmem = pl.BlockSpec(memory_space=pltpu.HBM), pl.BlockSpec(memory_space=pltpu.VMEM)
    with jax.named_scope("pack"):
        pieces = call(
            pack_kernel,
            pltpu.HBM((NORB, ROWS, LANES), jnp.float32),
            "pack",
            1 << 20,
            2 * mib,
            in_specs=[far],
            out_specs=far,
            scratch_shapes=[
                pltpu.VMEM((16, NY, NZ), jnp.float32),
                pltpu.VMEM((NORB, ROWS, LANES), jnp.float32),
                pltpu.SemaphoreType.DMA((2, XG)),
            ],
        )(pltpu.with_memory_space_constraint(orbitals[0], pltpu.HBM))
    with jax.named_scope("transpose"):
        arrived = exchange(pieces, ORB).reshape(NORB * ROWS, LANES)
    with jax.named_scope("owner"):
        slab = orbitals[0]
        below = shift(slab[16 - REACH :], COMP, 8, False)
        above = shift(slab[:REACH], COMP, 8, True)
        own, own_squares = call(owner_kernel, [f32(16, NY, NZ), f32(8, LANES)], "owner", 1 << 30, 4 * mib)(
            slab, below, above, potential, jnp.asarray(line_matrix())
        )
        depth = lax.broadcasted_iota(jnp.int32, (16, NY, NZ), 2)
        inside = ((depth >= segments[0][..., None]) & (depth < segments[1][..., None])).astype(jnp.float32)
    with jax.named_scope("block_constants"):
        place = jnp.stack([lax.axis_index("x"), lax.axis_index("z")]).astype(jnp.int32)
        smem = pl.BlockSpec(memory_space=pltpu.SMEM)
        diagonal = call(
            constants_kernel, f32(ROWS, LANES), "constants", 1 << 20, mib, in_specs=[smem, vmem]
        )(place, potential)
    arrived, diagonal, own, own_squares, inside = lax.optimization_barrier(
        (arrived, diagonal, own, own_squares, inside)
    )
    edge = edge_matrix()
    edge_high = edge.astype(jnp.bfloat16)
    edge_low = (edge - edge_high.astype(np.float64)).astype(jnp.bfloat16)

    whole = f32(ROWS, NORB, LANES)
    y_side, x_side, z_side = (f32(n, NORB, LANES) for n in (2 * REACH, 2 * REACH, YB))

    def send(kernel, kept_out, sides, name, *inputs):
        return call(
            kernel,
            kept_out + [pltpu.HBM(side.shape, jnp.float32) for side in sides],
            name,
            1 << 20,
            4 * mib,
            out_specs=[vmem] * len(kept_out) + [far] * len(sides),
            scratch_shapes=[pltpu.VMEM(side.shape, jnp.float32) for side in sides]
            + [pltpu.SemaphoreType.DMA((len(sides),))],
        )(*inputs)

    with jax.named_scope("spread"):
        ready, y_up_a, y_down_b = send(spread_y_kernel, [f32(8, LANES)], [y_side, y_side], "spread_y", arrived)
        phi, x_up, z_up = send(spread_kernel, [whole], [x_side, z_side], "spread", arrived, ready)
    with jax.named_scope("halo"):
        y_up_a = shift(y_up_a, "z", 16, True)
        y_down_b = shift(y_down_b, "z", 16, False)
        x_up = shift(x_up, COMP, 8, True)
        z_up = shift(z_up, "x", 4, True)
    with jax.named_scope("inner"):
        sums = call(inner_kernel, f32(NORB, NORB), "inner", 1 << 32, 2 * mib)(
            phi, diagonal, jnp.asarray(inner_blocks())
        )
    with jax.named_scope("edge"):
        partial = call(edge_kernel, f32(16 * FOLD, LANES), "edge", 1 << 31, 4 * mib)(
            phi, sums, jnp.asarray(edge_high), jnp.asarray(edge_low), y_up_a, y_down_b, x_up, z_up
        )
    with jax.named_scope("correlation_sum"):
        partial = exchange_folded(partial, ("z",))
        partial = call(functools.partial(sum_kernel, 16), f32(32 * FOLD, LANES), "sum_column", 1 << 16, mib)(partial)
        partial = exchange_folded(partial, ("core", "x", "y"))
    with jax.named_scope("mix"):
        sent, cross = call(
            mix_kernel,
            [f32(NORB * (ROWS + 1), LANES), f32(8, LANES)],
            "mix",
            1 << 28,
            3 * mib,
            in_specs=[vmem, vmem, smem, vmem],
        )(phi, partial, place, own_squares)
    with jax.named_scope("transpose_back"):
        back = exchange(sent.reshape(NORB, ROWS + 1, 1, LANES), ORB).reshape(NORB * (ROWS + 1), LANES)
    with jax.named_scope("rms"):
        sent = call(squares_kernel, f32(8, LANES), "squares", 1 << 14, 1 << 15)(back)
        terms = jnp.sum(exchange(sent.reshape(8, 1, LANES), COMP), axis=(0, 1))
        of_images = terms[NORB:]
        squares = of_images - 2.0 * cross[0, :NORB] + terms[:NORB]
    with jax.named_scope("finish"):
        new, direct = call(
            finish_kernel,
            [f32(16, NY, NZ), f32(8, LANES)],
            "finish",
            1 << 22,
            5 * mib,
            in_specs=[vmem, vmem, far, vmem],
            scratch_shapes=[pltpu.VMEM((16, NY, NZ), jnp.float32), pltpu.SemaphoreType.DMA((XG,))],
        )(back, slab, pltpu.with_memory_space_constraint(own, pltpu.HBM), inside)
    with jax.named_scope("rms"):

        def summed_directly():
            mine = jnp.broadcast_to(direct[0:1, :NORB], (NORB, NORB))
            lane = lax.broadcasted_iota(jnp.int32, (NORB, NORB), 1)
            mine = jnp.where(lane == place[0] * 16 + place[1], mine, 0.0)
            slabs = jnp.sum(exchange(mine, ORB), axis=0)
            return jnp.sum(exchange(jnp.broadcast_to(slabs, (8, NORB)), COMP), axis=0)

        cancels = jnp.logical_not(jnp.all(squares >= 0.03 * of_images))
        squares = lax.cond(cancels, summed_directly, lambda: squares)
        grad_rms = jnp.sqrt(squares / CELLS)
    return new[None], grad_rms


def solution(mesh):
    fine = Mesh(mesh.devices.reshape(4, 16, 4, 2), ("x", "z", "y", "core"))
    return jax.shard_map(
        on_device,
        mesh=fine,
        in_specs=(P(ORB, COMP, None, None), P(COMP, None, None), P(None, COMP, None)),
        out_specs=(P(ORB, COMP, None, None), P()),
        check_vma=False,
    )
```

```python
import functools
import math

import jax
import jax.numpy as jnp
import numpy as np
from jax import lax
from jax.experimental import pallas as pl
from jax.experimental.pallas import tpu as pltpu
from jax.sharding import Mesh
from jax.sharding import PartitionSpec as P

spacing = 0.4
descent = 0.02
NX, NY, NZ, NORB = 128, 128, 128, 64
CELLS = NX * NY * NZ
KINETIC = -0.5 / spacing**2
REACH = 7
XG, YB, XL, ZB = 4, 8, 4, 32
ROWS, LANES = XG * YB, XL * ZB
FOLD = 17
HIGH = lax.Precision.HIGHEST
PARAMS = pltpu.CompilerParams(vmem_limit_bytes=12 * 1024 * 1024)
ORB, COMP = ("x", "z"), ("y", "core")


def second_coefs_list():
    terms = []
    for k in range(1, REACH + 1):
        terms.append(
            2.0
            * (-1) ** (k + 1)
            * math.factorial(REACH) ** 2
            / (k * k * math.factorial(REACH - k) * math.factorial(REACH + k))
        )
    return [-2.0 * sum(terms)] + terms


COEFS = [KINETIC * c for c in second_coefs_list()]


def coef(k):
    return COEFS[k] if 1 <= k <= REACH else 0.0


def inner_blocks():
    steps = np.arange(XL)[:, None] - np.arange(XL)[None, :]
    line_z = np.array([[coef(abs(i - j)) for j in range(ZB)] for i in range(ZB)])
    blocks = []
    for shift_by in range(-2, 3):
        line_x = np.array([[coef(abs(int(s) - shift_by * XL)) for s in row] for row in steps])
        blocks.append(np.kron(line_x, np.eye(ZB)) + (np.kron(np.eye(XL), line_z) if shift_by == 0 else 0.0))
    return np.stack(blocks).astype(np.float32)


def edge_matrix():
    table = np.zeros((3 * LANES, XG * LANES))
    for x in range(16):
        for z in range(ZB):
            out = x * ZB + z
            for layer in range(8):
                table[layer * ZB + z, out] += coef(16 + layer - x)
            for t in range(8):
                table[2 * LANES + (x % XL) * ZB + (x // XL) * 8 + t, out] += coef(ZB + t - z)
    return table


def line_matrix():
    return np.array([[coef(abs(i - j)) for j in range(NZ)] for i in range(NZ)], np.float32)


def split(value):
    high = value.astype(jnp.bfloat16)
    return high, (value - high.astype(jnp.float32)).astype(jnp.bfloat16)


def three_products(left, right, dims=(((1,), (0,)), ((), ()))):
    def product(a, b):
        return lax.dot_general(a, b, dims, preferred_element_type=jnp.float32)

    return product(left[0], right[0]) + (product(left[1], right[0]) + product(left[0], right[1]))


def pack_kernel(slab, dst, src, out, sems):
    group = lax.broadcasted_iota(jnp.int32, (32, LANES), 1) // ZB
    comes, goes = [], []
    for xg in range(XG):
        layers, rows = pl.ds(xg * XL, XL), pl.ds(xg * YB, YB)
        comes.append(pltpu.make_async_copy(slab.at[layers], src.at[layers], sems.at[0, xg]))
        goes.append(pltpu.make_async_copy(out.at[:, rows], dst.at[:, rows], sems.at[1, xg]))
        comes[xg].start()
    for xg in range(XG):
        comes[xg].wait()
        for part in range(4):
            rows = slice(part * 32, part * 32 + 32)
            layers = [src[xg * XL + x, rows, :] for x in range(XL)]
            for q in range(4):
                piece = layers[q]
                for x in range(XL):
                    if x != q:
                        moved = pltpu.roll(layers[x], ((x - q) * ZB) % LANES, 1)
                        piece = jnp.where(group == x, moved, piece)
                first = q * 16 + part * 4
                out[first : first + 4, xg * YB : (xg + 1) * YB, :] = piece.reshape(4, YB, LANES)
        goes[xg].start()
    for move in goes:
        move.wait()


def finish_kernel(src, slab, images, inside, dst, squares, own, sems):
    group = lax.broadcasted_iota(jnp.int32, (YB, LANES), 1) // ZB
    total = jnp.zeros((YB, LANES), jnp.float32)
    moves = []
    for xg in range(XG):
        layers = pl.ds(xg * XL, XL)
        moves.append(pltpu.make_async_copy(images.at[layers], own.at[layers], sems.at[xg]))
        moves[xg].start()
    for xg in range(XG):
        moves[xg].wait()
        for yb in range(16):
            rows = slice(yb * YB, (yb + 1) * YB)
            pieces = [src[pl.ds((q * 16 + yb) * (ROWS + 1) + xg * YB, YB), :] for q in range(4)]
            for x in range(XL):
                mixed = pieces[x]
                for q in range(4):
                    if q != x:
                        moved = pltpu.roll(pieces[q], ((q - x) * ZB) % LANES, 1)
                        mixed = jnp.where(group == q, moved, mixed)
                layer = xg * XL + x
                gradient = own[layer, rows, :] - mixed
                total = total + gradient * gradient
                moved = slab[layer, rows, :] - descent * gradient
                dst[layer, rows, :] = jnp.where(inside[layer, rows, :] > 0.0, moved, 0.0)
    squares[...] = jnp.broadcast_to(jnp.sum(total, keepdims=True), squares.shape)


def owner_kernel(slab, below, above, potential, line, own, squares):
    total = jnp.zeros((NY, NZ), jnp.float32)
    for layer in range(16):
        here = slab[layer]
        value = (potential[layer] + jnp.float32(3.0 * COEFS[0])) * here
        value = value + jnp.dot(line[...], here, precision=HIGH, preferred_element_type=jnp.float32)
        value = value + jnp.dot(here, line[...], precision=HIGH, preferred_element_type=jnp.float32)
        for k in range(1, REACH + 1):
            up, down = layer + k, layer - k
            pair = (slab[up] if up < 16 else above[up - 16]) + (slab[down] if down >= 0 else below[down + REACH])
            value = value + COEFS[k] * pair
        own[layer] = value
        total = total + value * value
    squares[...] = jnp.broadcast_to(jnp.sum(total, keepdims=True), squares.shape)


def spread_y_kernel(src, ready, *refs):
    sent, kept, sems = refs[:2], refs[2:4], refs[4]
    ready[...] = jnp.zeros(ready.shape, jnp.float32)
    moves = [pltpu.make_async_copy(kept[side], sent[side], sems.at[side]) for side in range(2)]
    for xg in range(XG):
        for i in range(REACH):
            y = i if xg < 2 else i + 1
            kept[xg // 2][(xg % 2) * REACH + i] = src[pl.ds(xg * YB + y, NORB, stride=ROWS), :]
        if xg % 2:
            moves[xg // 2].start()
    for move in moves:
        move.wait()


def spread_kernel(src, ready, phi, *refs):
    sent, kept, sems = refs[:2], refs[2:4], refs[4]
    x_up, z_up = kept
    moves = [pltpu.make_async_copy(kept[i], sent[i], sems.at[i]) for i in range(2)]
    z_rows = [None] * YB
    lane = lax.broadcasted_iota(jnp.int32, (NORB, LANES), 1)
    slot = (lane % ZB) // 8
    for xg in range(XG):
        for y in range(YB):
            r = xg * YB + y
            row = src[pl.ds(r, NORB, stride=ROWS), :]
            phi[r] = row
            if xg == 0:
                x_up[r] = row
            up = pltpu.roll(row, xg * 8, 1) if xg else row
            z_rows[y] = jnp.where(slot == xg, up, z_rows[y]) if xg else up
        if xg == 1:
            for y in range(6):
                moved = pltpu.roll(phi[YB + 6 + y // 3], (XL - 1 - y % 3) * ZB, 1)
                x_up[YB + y] = jnp.where(lane >= (XL - 1) * ZB, moved, phi[YB + y])
            moves[0].start()
    for y in range(REACH):
        moved = pltpu.roll(z_rows[REACH], REACH - y, 1)
        z_up[y] = jnp.where(lane % 8 == REACH, moved, z_rows[y])
    moves[1].start()
    for move in moves:
        move.wait()


def constants_kernel(place, potential, diagonal):
    x_pos, z_pos = place[0], place[1]
    lane = lax.broadcasted_iota(jnp.int32, (YB, LANES), 1)
    first_row = pl.multiple_of(z_pos * YB, YB)
    for xg in range(XG):
        block = jnp.zeros((YB, LANES), jnp.float32)
        for x in range(XL):
            rows = potential[xg * XL + x, pl.ds(first_row, YB), :]
            moved = pltpu.roll(rows, lax.rem(x * ZB + LANES - x_pos * ZB, LANES), 1)
            block = jnp.where(lane // ZB == x, moved, block)
        diagonal[xg * YB : (xg + 1) * YB, :] = block + jnp.float32(3.0 * COEFS[0])


def tall(ref, xg):
    return ref[xg * YB : (xg + 1) * YB].reshape(YB * NORB, LANES)


def inner_kernel(phi, diagonal, blocks, sums):
    total = jnp.zeros((NORB, NORB), jnp.float32)
    nothing = jnp.zeros((LANES, LANES), jnp.float32)
    for pair in range(2):
        matrix = jnp.concatenate(
            [
                jnp.concatenate([blocks[to - xg + 2] if abs(to - xg) <= 2 else nothing for xg in range(XG)], axis=0)
                for to in (2 * pair, 2 * pair + 1)
            ],
            axis=1,
        )
        cells = jnp.concatenate([tall(phi, xg) for xg in range(XG)], axis=1)
        both = jnp.dot(cells, matrix, precision=HIGH, preferred_element_type=jnp.float32)
        for xg in (2 * pair, 2 * pair + 1):
            own = slice((xg % 2) * LANES, (xg % 2 + 1) * LANES)
            rows = [phi[xg * YB + y] for y in range(YB)]
            values = []
            for y in range(YB):
                r = xg * YB + y
                value = both[y * NORB : (y + 1) * NORB, own] + diagonal[r : r + 1, :] * rows[y]
                for other in range(YB):
                    if other != y:
                        value = value + COEFS[abs(other - y)] * rows[other]
                values.append(value)
            total = total + lax.dot_general(
                jnp.concatenate(rows, axis=1),
                jnp.concatenate(values, axis=1),
                (((1,), (1,)), ((), ())),
                precision=HIGH,
                preferred_element_type=jnp.float32,
            )
    sums[...] = total


def fold(table):
    n = NORB // 2
    above = lax.broadcasted_iota(jnp.int32, (n, n), 0) - lax.broadcasted_iota(jnp.int32, (n, n), 1)
    last = table[n:, n:]
    corner = table[:n, n:]
    mixed = jnp.where(above <= 0, table[:n, :n], last)
    diagonal = jnp.sum(jnp.where(above == 0, last, 0.0), axis=0, keepdims=True)
    top = jnp.concatenate([corner[: n // 2], corner[n // 2 :], mixed[: n // 2], mixed[n // 2 :]], axis=1)
    bottom = jnp.concatenate([diagonal, jnp.zeros((1, LANES - n), jnp.float32)], axis=1)
    return top, bottom


def unfold(top, bottom):
    n = NORB // 2
    above = lax.broadcasted_iota(jnp.int32, (n, n), 0) - lax.broadcasted_iota(jnp.int32, (n, n), 1)
    corner = jnp.concatenate([top[:, :n], top[:, n : 2 * n]], axis=0)
    mixed = jnp.concatenate([top[:, 2 * n : 3 * n], top[:, 3 * n :]], axis=0)
    turned = mixed.T
    first = jnp.where(above <= 0, mixed, turned)
    last = jnp.where(above > 0, mixed, jnp.where(above == 0, bottom[:, :n], turned))
    left = jnp.concatenate([first, corner.T], axis=0)
    right = jnp.concatenate([corner, last], axis=0)
    return jnp.concatenate([left, right], axis=1)


def edge_kernel(phi, sums, high, low, y_a, y_b, x_up, z_up, partial):
    total = sums[...]
    lane = lax.broadcasted_iota(jnp.int32, (NORB, LANES), 1)
    z_rows = [z_up[y] for y in range(REACH)]
    z_rows.append(z_rows[0])
    for y in range(REACH):
        z_rows[REACH] = jnp.where(lane % 8 == y, pltpu.roll(z_rows[y], LANES - (REACH - y), 1), z_rows[REACH])
    z_halo = jnp.stack(z_rows).reshape(YB * NORB, LANES)
    place = lax.broadcasted_iota(jnp.int32, (NORB, LANES), 1) // ZB
    next_rows = [x_up[YB + y] for y in range(6)]
    for y in (0, 3):
        parts = [pltpu.roll(next_rows[y + i], (i + 1) * ZB, 1) for i in range(3)]
        next_rows.append(jnp.where(place == 0, parts[0], jnp.where(place == 1, parts[1], parts[2])))
    next_group = jnp.stack(next_rows).reshape(YB * NORB, LANES)
    for pair in range(2):
        parts = [tall(x_up, 0), next_group, z_halo] if pair else [z_halo]
        halo = split(jnp.concatenate(parts, axis=1))
        used = slice(0 if pair else 2 * LANES, 3 * LANES), slice(pair * 2 * LANES, (pair + 1) * 2 * LANES)
        both = three_products(halo, (high[used], low[used]))
        y_halo = y_b if pair else y_a
        for xg in (2 * pair, 2 * pair + 1):
            own = slice((xg % 2) * LANES, (xg % 2 + 1) * LANES)
            rows = [y_halo[(xg % 2) * REACH + i] for i in range(REACH)]
            values = []
            for y in range(YB):
                value = both[y * NORB : (y + 1) * NORB, own]
                for i in range(REACH):
                    k = y + REACH - i if pair else YB + i - y
                    if 1 <= k <= REACH:
                        value = value + COEFS[k] * rows[i]
                values.append(value)
            left = split(jnp.concatenate([phi[xg * YB + y] for y in range(YB)], axis=1))
            right = split(jnp.concatenate(values, axis=1))
            total = total + 2.0 * three_products(left, right, (((1,), (1,)), ((), ())))
    top, bottom = fold(total + total.T)
    store_copies(partial, top, bottom)


def store_copies(sent, top, bottom):
    for i in range(sent.shape[0] // FOLD):
        sent[i * FOLD : i * FOLD + FOLD - 1, :] = top
        sent[i * FOLD + FOLD - 1 : (i + 1) * FOLD, :] = bottom


def added(came, count):
    size = came.shape[0] // count
    top = came[0 : FOLD - 1, :]
    bottom = came[FOLD - 1 : FOLD, :]
    for i in range(1, count):
        top = top + came[i * size : i * size + FOLD - 1, :]
        bottom = bottom + came[i * size + FOLD - 1 : i * size + FOLD, :]
    return top, bottom


def sum_kernel(count, came, sent):
    store_copies(sent, *added(came, count))


def mix_kernel(phi, sums, place, own_squares, out, cross):
    lag = unfold(*added(sums, 32)) * jnp.float32(0.5 / CELLS)
    squares = jnp.zeros((NORB, LANES), jnp.float32)
    for xg in range(XG):
        rows = [phi[xg * YB + y] for y in range(YB)]
        mixed = jnp.dot(lag, jnp.concatenate(rows, axis=1), precision=HIGH, preferred_element_type=jnp.float32)
        for y in range(YB):
            value = mixed[:, y * LANES : (y + 1) * LANES]
            squares = squares + value * value
            out[pl.ds(xg * YB + y, NORB, stride=ROWS + 1), :] = value
    across = (((1,), (1,)), ((), ()))
    ones = jnp.ones((8, LANES), jnp.float32)
    sums_row = lax.dot_general(ones, squares, across, precision=HIGH, preferred_element_type=jnp.float32)
    products = lax.dot_general(ones[:, :NORB], lag * lag, across, precision=HIGH, preferred_element_type=jnp.float32)
    lane = lax.broadcasted_iota(jnp.int32, (8, NORB), 1)
    images = jnp.where(lane == place[0] * 16 + place[1], own_squares[:, :NORB], 0.0)
    row = jnp.concatenate([sums_row, images], axis=1)
    out[pl.ds(ROWS, NORB, stride=ROWS + 1), :] = jnp.broadcast_to(row[0:1, :], (NORB, LANES))
    cross[...] = jnp.concatenate([products * jnp.float32(CELLS), jnp.zeros((8, LANES - NORB), jnp.float32)], axis=1)


def squares_kernel(src, sent):
    rows = src[pl.ds(ROWS, NORB, stride=ROWS + 1), :]
    sent[...] = jnp.broadcast_to(jnp.sum(rows, axis=0, keepdims=True), sent.shape)


def f32(*shape):
    return jax.ShapeDtypeStruct(shape, jnp.float32)


def call(kernel, out_shape, name, flops, nbytes, **more):
    return pl.pallas_call(
        kernel,
        out_shape=out_shape,
        compiler_params=PARAMS,
        name=name,
        cost_estimate=pl.CostEstimate(flops=flops, bytes_accessed=nbytes, transcendentals=0),
        **more,
    )


def exchange(value, axes):
    return lax.all_to_all(value, axes, 0, 0, tiled=True)


def exchange_folded(value, axes):
    shape = value.shape
    return exchange(value.reshape(shape[0] // FOLD, FOLD, 1, LANES), axes).reshape(shape)


def shift(value, axes, count, up):
    pairs = [(i + 1, i) if up else (i, i + 1) for i in range(count - 1)]
    return lax.ppermute(value, axes, pairs)


def on_device(orbitals, potential, segments):
    mib = 1 << 20
    far, vmem = pl.BlockSpec(memory_space=pltpu.HBM), pl.BlockSpec(memory_space=pltpu.VMEM)
    with jax.named_scope("pack"):
        pieces = call(
            pack_kernel,
            pltpu.HBM((NORB, ROWS, LANES), jnp.float32),
            "pack",
            1 << 20,
            2 * mib,
            in_specs=[far],
            out_specs=far,
            scratch_shapes=[
                pltpu.VMEM((16, NY, NZ), jnp.float32),
                pltpu.VMEM((NORB, ROWS, LANES), jnp.float32),
                pltpu.SemaphoreType.DMA((2, XG)),
            ],
        )(pltpu.with_memory_space_constraint(orbitals[0], pltpu.HBM))
    with jax.named_scope("transpose"):
        arrived = exchange(pieces, ORB).reshape(NORB * ROWS, LANES)
    with jax.named_scope("owner"):
        slab = orbitals[0]
        below = shift(slab[16 - REACH :], COMP, 8, False)
        above = shift(slab[:REACH], COMP, 8, True)
        own, own_squares = call(owner_kernel, [f32(16, NY, NZ), f32(8, LANES)], "owner", 1 << 30, 4 * mib)(
            slab, below, above, potential, jnp.asarray(line_matrix())
        )
        depth = lax.broadcasted_iota(jnp.int32, (16, NY, NZ), 2)
        inside = ((depth >= segments[0][..., None]) & (depth < segments[1][..., None])).astype(jnp.float32)
    with jax.named_scope("block_constants"):
        place = jnp.stack([lax.axis_index("x"), lax.axis_index("z")]).astype(jnp.int32)
        smem = pl.BlockSpec(memory_space=pltpu.SMEM)
        diagonal = call(
            constants_kernel, f32(ROWS, LANES), "constants", 1 << 20, mib, in_specs=[smem, vmem]
        )(place, potential)
    arrived, diagonal, own, own_squares, inside = lax.optimization_barrier(
        (arrived, diagonal, own, own_squares, inside)
    )
    edge = edge_matrix()
    edge_high = edge.astype(jnp.bfloat16)
    edge_low = (edge - edge_high.astype(np.float64)).astype(jnp.bfloat16)

    whole = f32(ROWS, NORB, LANES)
    y_side, x_side, z_side = (f32(n, NORB, LANES) for n in (2 * REACH, 2 * REACH, REACH))

    def send(kernel, kept_out, sides, name, *inputs):
        return call(
            kernel,
            kept_out + [pltpu.HBM(side.shape, jnp.float32) for side in sides],
            name,
            1 << 20,
            4 * mib,
            out_specs=[vmem] * len(kept_out) + [far] * len(sides),
            scratch_shapes=[pltpu.VMEM(side.shape, jnp.float32) for side in sides]
            + [pltpu.SemaphoreType.DMA((len(sides),))],
        )(*inputs)

    with jax.named_scope("spread"):
        ready, y_up_a, y_down_b = send(spread_y_kernel, [f32(8, LANES)], [y_side, y_side], "spread_y", arrived)
        phi, x_up, z_up = send(spread_kernel, [whole], [x_side, z_side], "spread", arrived, ready)
    with jax.named_scope("halo"):
        y_up_a = shift(y_up_a, "z", 16, True)
        y_down_b = shift(y_down_b, "z", 16, False)
        x_up = shift(x_up, COMP, 8, True)
        z_up = shift(z_up, "x", 4, True)
    with jax.named_scope("inner"):
        sums = call(inner_kernel, f32(NORB, NORB), "inner", 1 << 32, 2 * mib)(
            phi, diagonal, jnp.asarray(inner_blocks())
        )
    with jax.named_scope("edge"):
        partial = call(edge_kernel, f32(16 * FOLD, LANES), "edge", 1 << 31, 4 * mib)(
            phi, sums, jnp.asarray(edge_high), jnp.asarray(edge_low), y_up_a, y_down_b, x_up, z_up
        )
    with jax.named_scope("correlation_sum"):
        partial = exchange_folded(partial, ("z",))
        partial = call(functools.partial(sum_kernel, 16), f32(32 * FOLD, LANES), "sum_column", 1 << 16, mib)(partial)
        partial = exchange_folded(partial, ("core", "x", "y"))
    with jax.named_scope("mix"):
        sent, cross = call(
            mix_kernel,
            [f32(NORB * (ROWS + 1), LANES), f32(8, LANES)],
            "mix",
            1 << 28,
            3 * mib,
            in_specs=[vmem, vmem, smem, vmem],
        )(phi, partial, place, own_squares)
    with jax.named_scope("transpose_back"):
        back = exchange(sent.reshape(NORB, ROWS + 1, 1, LANES), ORB).reshape(NORB * (ROWS + 1), LANES)
    with jax.named_scope("rms"):
        sent = call(squares_kernel, f32(8, LANES), "squares", 1 << 14, 1 << 15)(back)
        terms = jnp.sum(exchange(sent.reshape(8, 1, LANES), COMP), axis=(0, 1))
        of_images = terms[NORB:]
        squares = of_images - 2.0 * cross[0, :NORB] + terms[:NORB]
    with jax.named_scope("finish"):
        new, direct = call(
            finish_kernel,
            [f32(16, NY, NZ), f32(8, LANES)],
            "finish",
            1 << 22,
            5 * mib,
            in_specs=[vmem, vmem, far, vmem],
            scratch_shapes=[pltpu.VMEM((16, NY, NZ), jnp.float32), pltpu.SemaphoreType.DMA((XG,))],
        )(back, slab, pltpu.with_memory_space_constraint(own, pltpu.HBM), inside)
    with jax.named_scope("rms"):

        def summed_directly():
            mine = jnp.broadcast_to(direct[0:1, :NORB], (NORB, NORB))
            lane = lax.broadcasted_iota(jnp.int32, (NORB, NORB), 1)
            mine = jnp.where(lane == place[0] * 16 + place[1], mine, 0.0)
            slabs = jnp.sum(exchange(mine, ORB), axis=0)
            whole_sums = jnp.sum(exchange(jnp.broadcast_to(slabs, (8, NORB)), COMP), axis=0)
            return jnp.sqrt(whole_sums / CELLS)

        cancels = jnp.logical_not(jnp.all(squares >= 0.1 * of_images))
        from_terms = jnp.sqrt(squares / CELLS)
        grad_rms = lax.cond(cancels, summed_directly, lambda: from_terms)
    return new[None], grad_rms


def solution(mesh):
    fine = Mesh(mesh.devices.reshape(4, 16, 4, 2), ("x", "z", "y", "core"))
    return jax.shard_map(
        on_device,
        mesh=fine,
        in_specs=(P(ORB, COMP, None, None), P(COMP, None, None), P(None, COMP, None)),
        out_specs=(P(ORB, COMP, None, None), P()),
        check_vma=False,
    )
```

```python
import functools
import math

import jax
import jax.numpy as jnp
import numpy as np
from jax import lax
from jax.experimental import pallas as pl
from jax.experimental.pallas import tpu as pltpu
from jax.sharding import Mesh
from jax.sharding import PartitionSpec as P

spacing = 0.4
descent = 0.02
NX, NY, NZ, NORB = 128, 128, 128, 64
CELLS = NX * NY * NZ
KINETIC = -0.5 / spacing**2
REACH = 7
XG, YB, XL, ZB = 4, 8, 4, 32
ROWS, LANES = XG * YB, XL * ZB
FOLD = 17
HIGH = lax.Precision.HIGHEST
PARAMS = pltpu.CompilerParams(vmem_limit_bytes=12 * 1024 * 1024)
ORB, COMP = ("x", "z"), ("y", "core")


def second_coefs_list():
    terms = []
    for k in range(1, REACH + 1):
        terms.append(
            2.0
            * (-1) ** (k + 1)
            * math.factorial(REACH) ** 2
            / (k * k * math.factorial(REACH - k) * math.factorial(REACH + k))
        )
    return [-2.0 * sum(terms)] + terms


COEFS = [KINETIC * c for c in second_coefs_list()]


def coef(k):
    return COEFS[k] if 1 <= k <= REACH else 0.0


def inner_blocks():
    steps = np.arange(XL)[:, None] - np.arange(XL)[None, :]
    line_z = np.array([[coef(abs(i - j)) for j in range(ZB)] for i in range(ZB)])
    blocks = []
    for shift_by in range(-2, 3):
        line_x = np.array([[coef(abs(int(s) - shift_by * XL)) for s in row] for row in steps])
        blocks.append(np.kron(line_x, np.eye(ZB)) + (np.kron(np.eye(XL), line_z) if shift_by == 0 else 0.0))
    return np.stack(blocks).astype(np.float32)


def edge_matrix():
    table = np.zeros((3 * LANES, XG * LANES))
    for x in range(16):
        for z in range(ZB):
            out = x * ZB + z
            for layer in range(8):
                table[layer * ZB + z, out] += coef(16 + layer - x)
            for t in range(8):
                table[2 * LANES + (x % XL) * ZB + (x // XL) * 8 + t, out] += coef(ZB + t - z)
    return table


def line_matrix():
    return np.array([[coef(abs(i - j)) for j in range(NZ)] for i in range(NZ)], np.float32)


def split(value):
    high = value.astype(jnp.bfloat16)
    return high, (value - high.astype(jnp.float32)).astype(jnp.bfloat16)


def three_products(left, right, dims=(((1,), (0,)), ((), ()))):
    def product(a, b):
        return lax.dot_general(a, b, dims, preferred_element_type=jnp.float32)

    return product(left[0], right[0]) + (product(left[1], right[0]) + product(left[0], right[1]))


def pack_kernel(slab, dst, src, out, sems):
    group = lax.broadcasted_iota(jnp.int32, (32, LANES), 1) // ZB
    comes, goes = [], []
    for xg in range(XG):
        layers, rows = pl.ds(xg * XL, XL), pl.ds(xg * YB, YB)
        comes.append(pltpu.make_async_copy(slab.at[layers], src.at[layers], sems.at[0, xg]))
        goes.append(pltpu.make_async_copy(out.at[:, rows], dst.at[:, rows], sems.at[1, xg]))
        comes[xg].start()
    for xg in range(XG):
        comes[xg].wait()
        for part in range(4):
            rows = slice(part * 32, part * 32 + 32)
            layers = [src[xg * XL + x, rows, :] for x in range(XL)]
            for q in range(4):
                piece = layers[q]
                for x in range(XL):
                    if x != q:
                        moved = pltpu.roll(layers[x], ((x - q) * ZB) % LANES, 1)
                        piece = jnp.where(group == x, moved, piece)
                first = q * 16 + part * 4
                out[first : first + 4, xg * YB : (xg + 1) * YB, :] = piece.reshape(4, YB, LANES)
        goes[xg].start()
    for move in goes:
        move.wait()


def finish_kernel(src, slab, images, inside, dst, squares, own, sems):
    group = lax.broadcasted_iota(jnp.int32, (YB, LANES), 1) // ZB
    total = jnp.zeros((YB, LANES), jnp.float32)
    moves = []
    for xg in range(XG):
        layers = pl.ds(xg * XL, XL)
        moves.append(pltpu.make_async_copy(images.at[layers], own.at[layers], sems.at[xg]))
        moves[xg].start()
    for xg in range(XG):
        moves[xg].wait()
        for yb in range(16):
            rows = slice(yb * YB, (yb + 1) * YB)
            pieces = [src[pl.ds((q * 16 + yb) * (ROWS + 1) + xg * YB, YB), :] for q in range(4)]
            for x in range(XL):
                mixed = pieces[x]
                for q in range(4):
                    if q != x:
                        moved = pltpu.roll(pieces[q], ((q - x) * ZB) % LANES, 1)
                        mixed = jnp.where(group == q, moved, mixed)
                layer = xg * XL + x
                gradient = own[layer, rows, :] - mixed
                total = total + gradient * gradient
                moved = slab[layer, rows, :] - descent * gradient
                dst[layer, rows, :] = jnp.where(inside[layer, rows, :] > 0.0, moved, 0.0)
    squares[...] = jnp.broadcast_to(jnp.sum(total, keepdims=True), squares.shape)


def owner_kernel(slab, below, above, potential, line, own, squares):
    total = jnp.zeros((NY, NZ), jnp.float32)
    for layer in range(16):
        here = slab[layer]
        value = (potential[layer] + jnp.float32(3.0 * COEFS[0])) * here
        value = value + jnp.dot(line[...], here, precision=HIGH, preferred_element_type=jnp.float32)
        value = value + jnp.dot(here, line[...], precision=HIGH, preferred_element_type=jnp.float32)
        for k in range(1, REACH + 1):
            up, down = layer + k, layer - k
            pair = (slab[up] if up < 16 else above[up - 16]) + (slab[down] if down >= 0 else below[down + REACH])
            value = value + COEFS[k] * pair
        own[layer] = value
        total = total + value * value
    squares[...] = jnp.broadcast_to(jnp.sum(total, keepdims=True), squares.shape)


def spread_y_kernel(src, ready, *refs):
    sent, kept, sems = refs[:2], refs[2:4], refs[4]
    ready[...] = jnp.zeros(ready.shape, jnp.float32)
    moves = [pltpu.make_async_copy(kept[side], sent[side], sems.at[side]) for side in range(2)]
    for xg in range(XG):
        for i in range(REACH):
            y = i if xg < 2 else i + 1
            kept[xg // 2][(xg % 2) * REACH + i] = src[pl.ds(xg * YB + y, NORB, stride=ROWS), :]
        if xg % 2:
            moves[xg // 2].start()
    for move in moves:
        move.wait()


def spread_kernel(src, ready, phi, *refs):
    sent, kept, sems = refs[:2], refs[2:4], refs[4]
    x_up, z_up = kept
    moves = [pltpu.make_async_copy(kept[i], sent[i], sems.at[i]) for i in range(2)]
    z_rows = [None] * YB
    lane = lax.broadcasted_iota(jnp.int32, (NORB, LANES), 1)
    slot = (lane % ZB) // 8
    for xg in range(XG):
        for y in range(YB):
            r = xg * YB + y
            row = src[pl.ds(r, NORB, stride=ROWS), :]
            phi[r] = row
            if xg == 0:
                x_up[r] = row
            up = pltpu.roll(row, xg * 8, 1) if xg else row
            z_rows[y] = jnp.where(slot == xg, up, z_rows[y]) if xg else up
        if xg == 1:
            for y in range(6):
                moved = pltpu.roll(phi[YB + 6 + y // 3], (XL - 1 - y % 3) * ZB, 1)
                x_up[YB + y] = jnp.where(lane >= (XL - 1) * ZB, moved, phi[YB + y])
            moves[0].start()
    for y in range(REACH):
        moved = pltpu.roll(z_rows[REACH], REACH - y, 1)
        z_up[y] = jnp.where(lane % 8 == REACH, moved, z_rows[y])
    moves[1].start()
    for move in moves:
        move.wait()


def constants_kernel(place, potential, diagonal):
    x_pos, z_pos = place[0], place[1]
    lane = lax.broadcasted_iota(jnp.int32, (YB, LANES), 1)
    first_row = pl.multiple_of(z_pos * YB, YB)
    for xg in range(XG):
        block = jnp.zeros((YB, LANES), jnp.float32)
        for x in range(XL):
            rows = potential[xg * XL + x, pl.ds(first_row, YB), :]
            moved = pltpu.roll(rows, lax.rem(x * ZB + LANES - x_pos * ZB, LANES), 1)
            block = jnp.where(lane // ZB == x, moved, block)
        diagonal[xg * YB : (xg + 1) * YB, :] = block + jnp.float32(3.0 * COEFS[0])


def tall(ref, xg):
    return ref[xg * YB : (xg + 1) * YB].reshape(YB * NORB, LANES)


def inner_kernel(phi, diagonal, blocks, sums):
    total = jnp.zeros((NORB, NORB), jnp.float32)
    nothing = jnp.zeros((LANES, LANES), jnp.float32)
    for pair in range(2):
        matrix = jnp.concatenate(
            [
                jnp.concatenate([blocks[to - xg + 2] if abs(to - xg) <= 2 else nothing for xg in range(XG)], axis=0)
                for to in (2 * pair, 2 * pair + 1)
            ],
            axis=1,
        )
        cells = jnp.concatenate([tall(phi, xg) for xg in range(XG)], axis=1)
        both = jnp.dot(cells, matrix, precision=HIGH, preferred_element_type=jnp.float32)
        for xg in (2 * pair, 2 * pair + 1):
            own = slice((xg % 2) * LANES, (xg % 2 + 1) * LANES)
            rows = [phi[xg * YB + y] for y in range(YB)]
            values = []
            for y in range(YB):
                r = xg * YB + y
                value = both[y * NORB : (y + 1) * NORB, own] + diagonal[r : r + 1, :] * rows[y]
                for other in range(YB):
                    if other != y:
                        value = value + COEFS[abs(other - y)] * rows[other]
                values.append(value)
            total = total + lax.dot_general(
                jnp.concatenate(rows, axis=1),
                jnp.concatenate(values, axis=1),
                (((1,), (1,)), ((), ())),
                precision=HIGH,
                preferred_element_type=jnp.float32,
            )
    sums[...] = total


def fold(table):
    n = NORB // 2
    above = lax.broadcasted_iota(jnp.int32, (n, n), 0) - lax.broadcasted_iota(jnp.int32, (n, n), 1)
    last = table[n:, n:]
    corner = table[:n, n:]
    mixed = jnp.where(above <= 0, table[:n, :n], last)
    diagonal = jnp.sum(jnp.where(above == 0, last, 0.0), axis=0, keepdims=True)
    top = jnp.concatenate([corner[: n // 2], corner[n // 2 :], mixed[: n // 2], mixed[n // 2 :]], axis=1)
    bottom = jnp.concatenate([diagonal, jnp.zeros((1, LANES - n), jnp.float32)], axis=1)
    return top, bottom


def unfold(top, bottom):
    n = NORB // 2
    above = lax.broadcasted_iota(jnp.int32, (n, n), 0) - lax.broadcasted_iota(jnp.int32, (n, n), 1)
    corner = jnp.concatenate([top[:, :n], top[:, n : 2 * n]], axis=0)
    mixed = jnp.concatenate([top[:, 2 * n : 3 * n], top[:, 3 * n :]], axis=0)
    turned = mixed.T
    first = jnp.where(above <= 0, mixed, turned)
    last = jnp.where(above > 0, mixed, jnp.where(above == 0, bottom[:, :n], turned))
    left = jnp.concatenate([first, corner.T], axis=0)
    right = jnp.concatenate([corner, last], axis=0)
    return jnp.concatenate([left, right], axis=1)


def edge_kernel(phi, sums, high, low, y_a, y_b, x_up, z_up, partial):
    total = sums[...]
    lane = lax.broadcasted_iota(jnp.int32, (NORB, LANES), 1)
    z_rows = [z_up[y] for y in range(REACH)]
    z_rows.append(z_rows[0])
    for y in range(REACH):
        z_rows[REACH] = jnp.where(lane % 8 == y, pltpu.roll(z_rows[y], LANES - (REACH - y), 1), z_rows[REACH])
    z_halo = jnp.stack(z_rows).reshape(YB * NORB, LANES)
    place = lax.broadcasted_iota(jnp.int32, (NORB, LANES), 1) // ZB
    next_rows = [x_up[YB + y] for y in range(6)]
    for y in (0, 3):
        parts = [pltpu.roll(next_rows[y + i], (i + 1) * ZB, 1) for i in range(3)]
        next_rows.append(jnp.where(place == 0, parts[0], jnp.where(place == 1, parts[1], parts[2])))
    next_group = jnp.stack(next_rows).reshape(YB * NORB, LANES)
    for pair in range(2):
        parts = [tall(x_up, 0), next_group, z_halo] if pair else [z_halo]
        halo = split(jnp.concatenate(parts, axis=1))
        used = slice(0 if pair else 2 * LANES, 3 * LANES), slice(pair * 2 * LANES, (pair + 1) * 2 * LANES)
        both = three_products(halo, (high[used], low[used]))
        y_halo = y_b if pair else y_a
        for xg in (2 * pair, 2 * pair + 1):
            own = slice((xg % 2) * LANES, (xg % 2 + 1) * LANES)
            rows = [y_halo[(xg % 2) * REACH + i] for i in range(REACH)]
            values = []
            for y in range(YB):
                value = both[y * NORB : (y + 1) * NORB, own]
                for i in range(REACH):
                    k = y + REACH - i if pair else YB + i - y
                    if 1 <= k <= REACH:
                        value = value + COEFS[k] * rows[i]
                values.append(value)
            left = split(jnp.concatenate([phi[xg * YB + y] for y in range(YB)], axis=1))
            right = split(jnp.concatenate(values, axis=1))
            total = total + 2.0 * three_products(left, right, (((1,), (1,)), ((), ())))
    top, bottom = fold(total + total.T)
    store_copies(partial, top, bottom)


def store_copies(sent, top, bottom):
    for i in range(sent.shape[0] // FOLD):
        sent[i * FOLD : i * FOLD + FOLD - 1, :] = top
        sent[i * FOLD + FOLD - 1 : (i + 1) * FOLD, :] = bottom


def added(came, count):
    size = came.shape[0] // count
    top = came[0 : FOLD - 1, :]
    bottom = came[FOLD - 1 : FOLD, :]
    for i in range(1, count):
        top = top + came[i * size : i * size + FOLD - 1, :]
        bottom = bottom + came[i * size + FOLD - 1 : i * size + FOLD, :]
    return top, bottom


def sum_kernel(count, came, sent):
    store_copies(sent, *added(came, count))


def mix_kernel(phi, sums, place, own_squares, out, cross):
    lag = unfold(*added(sums, 32)) * jnp.float32(0.5 / CELLS)
    squares = jnp.zeros((NORB, LANES), jnp.float32)
    for xg in range(XG):
        rows = [phi[xg * YB + y] for y in range(YB)]
        mixed = jnp.dot(lag, jnp.concatenate(rows, axis=1), precision=HIGH, preferred_element_type=jnp.float32)
        for y in range(YB):
            value = mixed[:, y * LANES : (y + 1) * LANES]
            squares = squares + value * value
            out[pl.ds(xg * YB + y, NORB, stride=ROWS + 1), :] = value
    across = (((1,), (1,)), ((), ()))
    ones = jnp.ones((8, LANES), jnp.float32)
    sums_row = lax.dot_general(ones, squares, across, precision=HIGH, preferred_element_type=jnp.float32)
    products = lax.dot_general(ones[:, :NORB], lag * lag, across, precision=HIGH, preferred_element_type=jnp.float32)
    lane = lax.broadcasted_iota(jnp.int32, (8, NORB), 1)
    images = jnp.where(lane == place[0] * 16 + place[1], own_squares[:, :NORB], 0.0)
    row = jnp.concatenate([sums_row, images], axis=1)
    out[pl.ds(ROWS, NORB, stride=ROWS + 1), :] = jnp.broadcast_to(row[0:1, :], (NORB, LANES))
    cross[...] = jnp.concatenate([products * jnp.float32(CELLS), jnp.zeros((8, LANES - NORB), jnp.float32)], axis=1)


def squares_kernel(src, sent):
    rows = src[pl.ds(ROWS, NORB, stride=ROWS + 1), :]
    sent[...] = jnp.broadcast_to(jnp.sum(rows, axis=0, keepdims=True), sent.shape)


def verdict_kernel(came, cross, rms, cancels):
    terms = jnp.sum(came[...], axis=0, keepdims=True)
    of_images = terms[:, NORB:]
    squares = of_images - 2.0 * cross[0:1, :NORB] + terms[:, :NORB]
    rms[...] = jnp.sqrt(jnp.maximum(squares, 0.0) * jnp.float32(1.0 / CELLS))
    kept = jnp.where(squares >= 0.1 * of_images, 0.0, 1.0)
    cancels[0, 0] = (jnp.sum(kept) > 0.0).astype(jnp.int32)


def f32(*shape):
    return jax.ShapeDtypeStruct(shape, jnp.float32)


def call(kernel, out_shape, name, flops, nbytes, **more):
    return pl.pallas_call(
        kernel,
        out_shape=out_shape,
        compiler_params=PARAMS,
        name=name,
        cost_estimate=pl.CostEstimate(flops=flops, bytes_accessed=nbytes, transcendentals=0),
        **more,
    )


def exchange(value, axes):
    return lax.all_to_all(value, axes, 0, 0, tiled=True)


def exchange_folded(value, axes):
    shape = value.shape
    return exchange(value.reshape(shape[0] // FOLD, FOLD, 1, LANES), axes).reshape(shape)


def shift(value, axes, count, up):
    pairs = [(i + 1, i) if up else (i, i + 1) for i in range(count - 1)]
    return lax.ppermute(value, axes, pairs)


def on_device(orbitals, potential, segments):
    mib = 1 << 20
    far, vmem = pl.BlockSpec(memory_space=pltpu.HBM), pl.BlockSpec(memory_space=pltpu.VMEM)
    with jax.named_scope("pack"):
        pieces = call(
            pack_kernel,
            pltpu.HBM((NORB, ROWS, LANES), jnp.float32),
            "pack",
            1 << 20,
            2 * mib,
            in_specs=[far],
            out_specs=far,
            scratch_shapes=[
                pltpu.VMEM((16, NY, NZ), jnp.float32),
                pltpu.VMEM((NORB, ROWS, LANES), jnp.float32),
                pltpu.SemaphoreType.DMA((2, XG)),
            ],
        )(pltpu.with_memory_space_constraint(orbitals[0], pltpu.HBM))
    with jax.named_scope("transpose"):
        arrived = exchange(pieces, ORB).reshape(NORB * ROWS, LANES)
    with jax.named_scope("owner"):
        slab = orbitals[0]
        below = shift(slab[16 - REACH :], COMP, 8, False)
        above = shift(slab[:REACH], COMP, 8, True)
        own, own_squares = call(owner_kernel, [f32(16, NY, NZ), f32(8, LANES)], "owner", 1 << 30, 4 * mib)(
            slab, below, above, potential, jnp.asarray(line_matrix())
        )
        depth = lax.broadcasted_iota(jnp.int32, (16, NY, NZ), 2)
        inside = ((depth >= segments[0][..., None]) & (depth < segments[1][..., None])).astype(jnp.float32)
    with jax.named_scope("block_constants"):
        place = jnp.stack([lax.axis_index("x"), lax.axis_index("z")]).astype(jnp.int32)
        smem = pl.BlockSpec(memory_space=pltpu.SMEM)
        diagonal = call(
            constants_kernel, f32(ROWS, LANES), "constants", 1 << 20, mib, in_specs=[smem, vmem]
        )(place, potential)
    arrived, diagonal, own, own_squares, inside = lax.optimization_barrier(
        (arrived, diagonal, own, own_squares, inside)
    )
    edge = edge_matrix()
    edge_high = edge.astype(jnp.bfloat16)
    edge_low = (edge - edge_high.astype(np.float64)).astype(jnp.bfloat16)

    whole = f32(ROWS, NORB, LANES)
    y_side, x_side, z_side = (f32(n, NORB, LANES) for n in (2 * REACH, 2 * REACH, REACH))

    def send(kernel, kept_out, sides, name, *inputs):
        return call(
            kernel,
            kept_out + [pltpu.HBM(side.shape, jnp.float32) for side in sides],
            name,
            1 << 20,
            4 * mib,
            out_specs=[vmem] * len(kept_out) + [far] * len(sides),
            scratch_shapes=[pltpu.VMEM(side.shape, jnp.float32) for side in sides]
            + [pltpu.SemaphoreType.DMA((len(sides),))],
        )(*inputs)

    with jax.named_scope("spread"):
        ready, y_up_a, y_down_b = send(spread_y_kernel, [f32(8, LANES)], [y_side, y_side], "spread_y", arrived)
        phi, x_up, z_up = send(spread_kernel, [whole], [x_side, z_side], "spread", arrived, ready)
    with jax.named_scope("halo"):
        y_up_a = shift(y_up_a, "z", 16, True)
        y_down_b = shift(y_down_b, "z", 16, False)
        x_up = shift(x_up, COMP, 8, True)
        z_up = shift(z_up, "x", 4, True)
    with jax.named_scope("inner"):
        sums = call(inner_kernel, f32(NORB, NORB), "inner", 1 << 32, 2 * mib)(
            phi, diagonal, jnp.asarray(inner_blocks())
        )
    with jax.named_scope("edge"):
        partial = call(edge_kernel, f32(16 * FOLD, LANES), "edge", 1 << 31, 4 * mib)(
            phi, sums, jnp.asarray(edge_high), jnp.asarray(edge_low), y_up_a, y_down_b, x_up, z_up
        )
    with jax.named_scope("correlation_sum"):
        partial = exchange_folded(partial, ("z",))
        partial = call(functools.partial(sum_kernel, 16), f32(32 * FOLD, LANES), "sum_column", 1 << 16, mib)(partial)
        partial = exchange_folded(partial, ("core", "x", "y"))
    with jax.named_scope("mix"):
        sent, cross = call(
            mix_kernel,
            [f32(NORB * (ROWS + 1), LANES), f32(8, LANES)],
            "mix",
            1 << 28,
            3 * mib,
            in_specs=[vmem, vmem, smem, vmem],
        )(phi, partial, place, own_squares)
    with jax.named_scope("transpose_back"):
        back = exchange(sent.reshape(NORB, ROWS + 1, 1, LANES), ORB).reshape(NORB * (ROWS + 1), LANES)
    with jax.named_scope("rms"):
        sent = call(squares_kernel, f32(8, LANES), "squares", 1 << 14, 1 << 15)(back)
        came = exchange(sent.reshape(8, 1, LANES), COMP).reshape(8, LANES)
        from_terms, cancels = call(
            verdict_kernel,
            [f32(1, NORB), jax.ShapeDtypeStruct((1, 1), jnp.int32)],
            "verdict",
            1 << 12,
            1 << 13,
            out_specs=[vmem, smem],
        )(came, cross)
    with jax.named_scope("finish"):
        new, direct = call(
            finish_kernel,
            [f32(16, NY, NZ), f32(8, LANES)],
            "finish",
            1 << 22,
            5 * mib,
            in_specs=[vmem, vmem, far, vmem],
            scratch_shapes=[pltpu.VMEM((16, NY, NZ), jnp.float32), pltpu.SemaphoreType.DMA((XG,))],
        )(back, slab, pltpu.with_memory_space_constraint(own, pltpu.HBM), inside)
    with jax.named_scope("rms"):

        def summed_directly():
            mine = jnp.broadcast_to(direct[0:1, :NORB], (NORB, NORB))
            lane = lax.broadcasted_iota(jnp.int32, (NORB, NORB), 1)
            mine = jnp.where(lane == place[0] * 16 + place[1], mine, 0.0)
            slabs = jnp.sum(exchange(mine, ORB), axis=0)
            whole_sums = jnp.sum(exchange(jnp.broadcast_to(slabs, (8, NORB)), COMP), axis=0)
            return jnp.sqrt(whole_sums / CELLS)

        grad_rms = lax.cond(cancels[0, 0] > 0, summed_directly, lambda: from_terms[0])
    return new[None], grad_rms


def solution(mesh):
    fine = Mesh(mesh.devices.reshape(4, 16, 4, 2), ("x", "z", "y", "core"))
    return jax.shard_map(
        on_device,
        mesh=fine,
        in_specs=(P(ORB, COMP, None, None), P(COMP, None, None), P(None, COMP, None)),
        out_specs=(P(ORB, COMP, None, None), P()),
        check_vma=False,
    )
```
